32 devices in a mesh: aux: 2 (over y), ao: 16 (over z, x, core).
Axes of the slice: x: 2, y: 2, z: 4, core: 2. Of those that a mesh axis runs over, the one named last changes fastest.
Arguments:
- blocks: bfloat16 [64, 4000, 4000], P('aux', 'ao'), may hold values from -6 to 6
- block_scale: float32 [64, 160], P('aux', 'ao'), may hold values from 0.3 to 3
- coeff: bfloat16 [4000, 380], P('ao'), may hold values from -0.09375 to 0.09375
- rot_coeff: bfloat16 [4000, 380], P('ao'), may hold values from -0.09375 to 0.09375
- occupation: float32 [380], replicated, may hold values from 0.2 to 2
Outputs:
- sigma: float32 [4000, 380], P('ao')
The draws below stay inside these ranges and needn't reach their ends.
All inputs are finite; a program needn't handle non-finite values.
Results may differ from the reference program's by a relative error of at most 0.005.
Values may be sent and summed in bfloat16 or wider, within the bound.
No kernel may reach another device: no remote copies, remote signals or barrier semaphores. Data moves between devices by JAX's collectives and lax.ppermute only.
A program may use at most 256 MiB of HBM per device.

```python
import math
import jax
import jax.numpy as jnp
from jax import lax

NAO = 4000
RB = 25
NAUX = 64
NI = 380


def steps_of(stream_key, dims, split, low, largest):
    gain, own = 1.0, jax.random.fold_in(stream_key, 6)
    for dim, blocks in split:
        steps = jnp.exp(jax.random.uniform(jax.random.fold_in(own, dim), (blocks,), jnp.float32, low / len(split), largest / len(split)))
        gain = gain * jnp.repeat(steps, dims[dim] // blocks).reshape([-1 if axis == dim else 1 for axis in range(len(dims))])
    return gain


def bell_draw(own_key, extent, scale, bound, cuts=(), dtype=jnp.bfloat16):
    drawn = scale * jax.random.normal(own_key, extent, jnp.float32)
    if cuts:
        drawn = drawn * steps_of(own_key, extent, cuts, -0.22, 0.18)
    return jnp.clip(drawn, -bound, bound).astype(dtype)


def setup_inputs(seed: int = 0) -> dict:
    seeds = jax.random.split(jax.random.key(seed), 6)
    blocks = bell_draw(seeds[0], (NAUX, NAO, NAO), 1.0, 6.0, ((0, 2), (1, 16)))
    block_scale = jnp.clip(jnp.exp(math.log(3.0) - 2.3025851 * jax.random.uniform(seeds[1], (NAUX, NAO // RB), jnp.float32) ** steps_of(seeds[1], (NAUX, NAO // RB), ((0, 2), (1, 16)), -0.2, 0.2)), 0.3, 3.0)
    coeff = bell_draw(seeds[2], (NAO, NI), NAO ** -0.5, 0.09375, ((0, 16),))
    rot_coeff = bell_draw(seeds[3], (NAO, NI), NAO ** -0.5, 0.09375, ((0, 16),))
    occupation = jnp.clip(jax.random.uniform(seeds[4], (NI,), jnp.float32, 0.2, 2.0), 0.2, 2.0)
    return {"blocks": blocks, "block_scale": block_scale, "coeff": coeff, "rot_coeff": rot_coeff, "occupation": occupation}


def reference(blocks, block_scale, coeff, rot_coeff, occupation):
    both = jnp.concatenate([coeff, rot_coeff], axis=1)
    weighted = coeff.astype(jnp.float32) * occupation[None, :]

    def per_aux(item):
        block, scale_row = item
        half = jnp.dot(block, both, preferred_element_type=jnp.float32)
        half = half * jnp.repeat(scale_row, RB)[:, None]
        h_occ = half[:, :NI].astype(jnp.bfloat16)
        h_rot = half[:, NI:].astype(jnp.bfloat16)
        gamma = jnp.sum(h_rot.astype(jnp.float32) * weighted)
        ymo = jnp.dot(coeff.T, h_rot, preferred_element_type=jnp.float32).astype(jnp.bfloat16)
        return (h_occ, ymo, gamma)
    h_occ, ymo, gamma = lax.map(per_aux, (blocks, block_scale))
    flat_occ = h_occ.transpose(1, 0, 2).reshape(NAO, NAUX * NI)
    kterm = jnp.dot(flat_occ, ymo.reshape(NAUX * NI, NI), preferred_element_type=jnp.float32)
    jterm = jnp.einsum('p,pmi->mi', gamma, h_occ.astype(jnp.float32))
    return (2.0 * jterm - kterm) / jnp.sqrt(jnp.float32(NAUX * NI))
```

```python
import functools
import math

import jax
import jax.numpy as jnp
from jax import lax
from jax.experimental import pallas as pl
from jax.experimental.pallas import tpu as pltpu
from jax.sharding import PartitionSpec as P

BF16, F32 = jnp.bfloat16, jnp.float32
VMEM_BYTES = 50 * 2**20
LANES = 128


def up_to(value, step):
    return -(-value // step) * step


def layout_of(groups):
    core = 2 if groups % 2 == 0 else 1
    chips = groups // core
    x = 1
    while 4 * x * x <= chips and chips % (2 * x) == 0:
        x *= 2
    return chips // x, x, core


def rows_times(b_ref, m_ref, scale_ref, h_ref):
    mub, paux, naos = b_ref.shape
    step = pl.program_id(0)
    h = jnp.dot(b_ref[...].reshape(mub * paux, naos), m_ref[...], preferred_element_type=F32)
    h = h.reshape(mub, paux, -1) * scale_ref[...]
    h = h.reshape(mub * paux, -1).astype(BF16).astype(F32)
    first = pl.multiple_of(step * (mub * paux), 8)
    for t in range(h_ref.shape[0]):
        h_ref[t, pl.ds(first, mub * paux), :] = h[:, t * LANES : (t + 1) * LANES]


def rows_of(h_ref, p, paux):
    rows = h_ref.shape[1] // paux
    return jnp.concatenate(
        [h_ref[t, pl.ds(p, rows, stride=paux), :] for t in range(h_ref.shape[0])], axis=1
    )


def rot_kernel(paux, fan, subs, me_ref, b_ref, m_ref, scale_ref, ct_ref, w_ref, *rest):
    outs, gamma_ref, h_ref = rest[:-2], rest[-2], rest[-1]
    rows_times(b_ref, m_ref, scale_ref, h_ref)

    @pl.when(pl.program_id(0) == pl.num_programs(0) - 1)
    def _():
        each = paux // fan
        per = each // subs
        me = me_ref[0]
        for d in range(fan):
            base = jnp.bitwise_xor(me, d) * each
            for j in range(each):
                p = base + j
                hp = rows_of(h_ref, p, paux)
                gamma_ref[pl.ds(p, 1)] = jnp.sum(hp * w_ref[...], axis=0, keepdims=True)[None]
                y = jnp.dot(ct_ref[...], hp.astype(BF16), preferred_element_type=F32)
                outs[d * subs + j // per][j % per] = y.astype(BF16)


def occ_kernel(paux, b_ref, m_ref, scale_ref, out_ref, h_ref):
    rows_times(b_ref, m_ref, scale_ref, h_ref)

    @pl.when(pl.program_id(0) == pl.num_programs(0) - 1)
    def _():
        for p in range(paux):
            out_ref[p] = rows_of(h_ref, p, paux).astype(BF16)


def sigma_kernel(fan, each, per, first, me_ref, gamma_ref, base_ref, *rest):
    h_refs, y_refs, out_ref = rest[:fan], rest[fan:-1], rest[-1]
    step = pl.program_id(0)

    @pl.when(step == 0)
    def _():
        out_ref[...] = base_ref[...]

    acc = out_ref[...]
    for d in range(fan):
        p = jnp.bitwise_xor(me_ref[0], d) * each + first + step
        h = h_refs[d][0]
        acc = acc + (2.0 * gamma_ref[p]) * h.astype(F32)
        acc = acc - jnp.dot(h, y_refs[d][0], preferred_element_type=F32)
    out_ref[...] = acc


def block_specs(rows, nscale, paux, naos, width, chunk):
    mub = rows // nscale
    return [
        pl.BlockSpec((mub, paux, naos), lambda s, *_: (s, chunk, 0)),
        pl.BlockSpec((naos, width), lambda s, *_: (0, 0), pipeline_mode=pl.Buffered(1)),
        pl.BlockSpec((1, paux, 1), lambda s, *_: (s, chunk, 0)),
    ]


def rot_part(me, blocks, matrix, scale, ct, weighted, chunk, paux, fan, subs):
    rows, _, naos = blocks.shape
    nscale, width = scale.shape[0], matrix.shape[1]
    per = paux // fan // subs
    piece = jax.ShapeDtypeStruct((per, width, width), BF16)
    whole = lambda shape: pl.BlockSpec(shape, lambda s, *_: (0,) * len(shape))
    return pl.pallas_call(
        functools.partial(rot_kernel, paux, fan, subs),
        grid_spec=pltpu.PrefetchScalarGridSpec(
            num_scalar_prefetch=1,
            grid=(nscale,),
            in_specs=block_specs(rows, nscale, paux, naos, width, chunk)
            + [whole(ct.shape), whole(weighted.shape)],
            out_specs=[whole(piece.shape)] * (fan * subs) + [whole((paux, 1, width))],
            scratch_shapes=[pltpu.VMEM((width // LANES, rows * paux, LANES), F32)],
        ),
        out_shape=[piece] * (fan * subs) + [jax.ShapeDtypeStruct((paux, 1, width), F32)],
        compiler_params=pltpu.CompilerParams(vmem_limit_bytes=VMEM_BYTES),
        cost_estimate=pl.CostEstimate(
            flops=2 * rows * paux * naos * width, bytes_accessed=2 * rows * paux * naos, transcendentals=0
        ),
    )(me, blocks, matrix, scale, ct, weighted)


def occ_part(blocks, matrix, scale, chunk, paux):
    rows, _, naos = blocks.shape
    nscale, width = scale.shape[0], matrix.shape[1]
    return pl.pallas_call(
        functools.partial(occ_kernel, paux),
        grid=(nscale,),
        in_specs=block_specs(rows, nscale, paux, naos, width, chunk),
        out_specs=pl.BlockSpec((paux, rows, width), lambda s: (0, 0, 0)),
        out_shape=jax.ShapeDtypeStruct((paux, rows, width), BF16),
        scratch_shapes=[pltpu.VMEM((width // LANES, rows * paux, LANES), F32)],
        compiler_params=pltpu.CompilerParams(vmem_limit_bytes=VMEM_BYTES),
        cost_estimate=pl.CostEstimate(
            flops=2 * rows * paux * naos * width, bytes_accessed=2 * rows * paux * naos, transcendentals=0
        ),
    )(blocks, matrix, scale)


def sigma_part(me, gamma, base, h_occ, pieces, each, first):
    fan = len(pieces)
    per, width, _ = pieces[0].shape
    rows = h_occ.shape[1]

    def pick(d):
        return lambda s, me_ref: (jnp.bitwise_xor(me_ref[0], d) * each + first + s, 0, 0)

    return pl.pallas_call(
        functools.partial(sigma_kernel, fan, each, per, first),
        grid_spec=pltpu.PrefetchScalarGridSpec(
            num_scalar_prefetch=1,
            grid=(per,),
            in_specs=[
                pl.BlockSpec(memory_space=pltpu.SMEM),
                pl.BlockSpec((rows, width), lambda s, *_: (0, 0)),
            ]
            + [pl.BlockSpec((1, rows, width), pick(d)) for d in range(fan)]
            + [pl.BlockSpec((1, width, width), lambda s, *_: (s, 0, 0))] * fan,
            out_specs=pl.BlockSpec((rows, width), lambda s, *_: (0, 0)),
        ),
        out_shape=jax.ShapeDtypeStruct((rows, width), F32),
        compiler_params=pltpu.CompilerParams(vmem_limit_bytes=VMEM_BYTES),
        cost_estimate=pl.CostEstimate(
            flops=2 * fan * per * rows * width * width,
            bytes_accessed=4 * fan * per * width * width,
            transcendentals=0,
        ),
    )(me, gamma, base, *([h_occ] * fan), *pieces)


def body(blocks, block_scale, coeff, rot_coeff, occupation):
    groups, parts = lax.axis_size("ao"), lax.axis_size("aux")
    nz, nx, ncore = layout_of(groups)
    fan = nx * ncore
    naux, rows, naos = blocks.shape
    nint = coeff.shape[1]
    width = up_to(nint, LANES)
    index = lax.axis_index("ao")
    z = index // fan
    me = jnp.reshape(index % fan, (1,)).astype(jnp.int32)

    def swap(value, bit):
        return lax.ppermute(value, "ao", [(i, i ^ bit) for i in range(groups)])

    def along_z(value, pairs):
        return lax.ppermute(
            value, "ao", [(a * fan + i, b * fan + i) for a, b in pairs for i in range(fan)]
        )

    def sum_z(value):
        half = nz // 2
        inward = [[(k, k + 1), (nz - 1 - k, nz - 2 - k)] for k in range(half - 1)]
        for pairs in inward:
            value = value + along_z(value, pairs)
        if nz > 1:
            value = value + along_z(value, [(half - 1, half), (half, half - 1)])
        for pairs in reversed(inward):
            got = along_z(value, [(b, a) for a, b in pairs])
            outer = functools.reduce(jnp.logical_or, [z == a for a, _ in pairs])
            value = jnp.where(outer, got, value)
        return value

    def reduce_all(pieces):
        bit = 1
        bits = []
        live = list(range(fan))
        while bit < fan:
            bits.append(bit)
            sent = {d: swap(pieces[d], bit) for d in live if d & bit}
            live = [d for d in live if not d & bit]
            pieces = {d: pieces[d] + sent[d | bit] for d in live}
            bit *= 2
        total = {0: sum_z(pieces[0])}
        for bit in reversed(bits):
            total.update({d | bit: swap(v, bit) for d, v in list(total.items())})
        return [total[d] for d in range(fan)]

    def gathered(local):
        whole = lax.all_gather(local, "ao", axis=0, tiled=True)
        return jnp.pad(whole, ((0, 0), (0, width - nint)))

    paux = 16 if naux % 16 == 0 else naux
    chunks = naux // paux
    each = paux // fan
    subs = 2 if each % 2 == 0 else 1
    per = each // subs

    by_rows = blocks.transpose(1, 0, 2)
    scale = block_scale.T[:, :, None]
    ct = jnp.pad(coeff.T, ((0, width - nint), (0, 0)))
    weighted = jnp.pad(coeff.astype(F32) * occupation[None, :], ((0, 0), (0, width - nint)))
    whole_r = gathered(rot_coeff)
    whole_c = gathered(coeff)

    pieces, gammas = [], []
    for c in range(chunks):
        *out, g = rot_part(me, by_rows, whole_r, scale, ct, weighted, c, paux, fan, subs)
        pieces.append(out)
        gammas.append(g)
    gamma = lax.psum(jnp.sum(jnp.concatenate(gammas, axis=0), axis=(1, 2)), "ao")
    totals = [
        [reduce_all({d: pieces[c][d * subs + u] for d in range(fan)}) for u in range(subs)]
        for c in range(chunks)
    ]
    h_occ = [occ_part(by_rows, whole_c, scale, c, paux) for c in range(chunks)]
    sigma = jnp.zeros((rows, width), F32)
    for c in range(chunks):
        for u in range(subs):
            sigma = sigma_part(
                me, gamma[c * paux : (c + 1) * paux], sigma, h_occ[c], totals[c][u], each, u * per
            )
    bit = 1
    while bit < parts:
        sigma = sigma + lax.ppermute(sigma, "aux", [(i, i ^ bit) for i in range(parts)])
        bit *= 2
    return sigma[:, :nint] / math.sqrt(naux * parts * nint)


def solution(mesh):
    in_specs = (P("aux", "ao", None), P("aux", "ao"), P("ao", None), P("ao", None), P())
    out_specs = P("ao", None)
    return jax.shard_map(body, mesh=mesh, in_specs=in_specs, out_specs=out_specs, check_vma=False)
```

```python
import functools
import math

import jax
import jax.numpy as jnp
from jax import lax
from jax.experimental import pallas as pl
from jax.experimental.pallas import tpu as pltpu
from jax.sharding import PartitionSpec as P

BF16, F32 = jnp.bfloat16, jnp.float32
VMEM_BYTES = 50 * 2**20
LANES = 128


def up_to(value, step):
    return -(-value // step) * step


def layout_of(groups):
    core = 2 if groups % 2 == 0 else 1
    chips = groups // core
    x = 1
    while 4 * x * x <= chips and chips % (2 * x) == 0:
        x *= 2
    return chips // x, x, core


def rows_times(b_ref, m_ref, scale_ref, h_ref):
    mub, paux, naos = b_ref.shape
    step = pl.program_id(0)
    h = jnp.dot(b_ref[...].reshape(mub * paux, naos), m_ref[...], preferred_element_type=F32)
    h = h.reshape(mub, paux, -1) * scale_ref[...]
    h = h.reshape(mub * paux, -1).astype(BF16).astype(F32)
    first = pl.multiple_of(step * (mub * paux), 8)
    for t in range(h_ref.shape[0]):
        h_ref[t, pl.ds(first, mub * paux), :] = h[:, t * LANES : (t + 1) * LANES]


def rows_of(h_ref, p, paux):
    rows = h_ref.shape[1] // paux
    return jnp.concatenate(
        [h_ref[t, pl.ds(p, rows, stride=paux), :] for t in range(h_ref.shape[0])], axis=1
    )


def rot_kernel(paux, fan, nz, cuts, me_ref, b_ref, m_ref, scale_ref, ct_ref, w_ref, tie_ref, *rest):
    outs, gamma_ref, h_ref = rest[:fan], rest[fan], rest[fan + 1]
    rows_times(b_ref, m_ref, scale_ref, h_ref)

    @pl.when(pl.program_id(0) == pl.num_programs(0) - 1)
    def _():
        width = ct_ref.shape[0]
        shard = width // cuts
        for d in range(0, fan, cuts):
            wide = []
            for k in range(nz):
                p = (k * fan + jnp.bitwise_xor(me_ref[0], d)) // cuts
                hp = rows_of(h_ref, p, paux)
                gamma_ref[pl.ds(p, 1)] = jnp.sum(hp * w_ref[...], axis=0, keepdims=True)[None]
                wide.append(hp.astype(BF16))
            y = jnp.dot(ct_ref[...], jnp.concatenate(wide, axis=1), preferred_element_type=F32)
            y = y.astype(BF16)
            for k in range(nz):
                for e in range(cuts):
                    outs[d + e][k] = y[e * shard : (e + 1) * shard, k * width : (k + 1) * width]


def occ_kernel(paux, b_ref, m_ref, scale_ref, tie_ref, out_ref, h_ref):
    rows_times(b_ref, m_ref, scale_ref, h_ref)

    @pl.when(pl.program_id(0) == pl.num_programs(0) - 1)
    def _():
        for p in range(paux):
            out_ref[p] = rows_of(h_ref, p, paux).astype(BF16)


def sigma_kernel(batch, gamma_ref, base_ref, h_ref, y_ref, out_ref):
    step = pl.program_id(0)

    @pl.when(step == 0)
    def _():
        out_ref[...] = base_ref[...]

    h = jnp.concatenate([h_ref[b] for b in range(batch)], axis=1)
    y = y_ref[...].reshape(-1, y_ref.shape[2])
    acc = out_ref[...] - jnp.dot(h, y, preferred_element_type=F32)
    for b in range(batch):
        acc = acc + (2.0 * gamma_ref[step * batch + b]) * h_ref[b].astype(F32)
    out_ref[...] = acc


def cost(flops, nbytes):
    return pl.CostEstimate(flops=flops, bytes_accessed=nbytes, transcendentals=0)


def block_specs(rows, nscale, paux, naos, width, chunk):
    mub = rows // nscale
    return [
        pl.BlockSpec((mub, paux, naos), lambda s, *_: (s, chunk, 0)),
        pl.BlockSpec((naos, width), lambda s, *_: (0, 0), pipeline_mode=pl.Buffered(1)),
        pl.BlockSpec((1, paux, 1), lambda s, *_: (s, chunk, 0)),
    ]


def rot_part(me, blocks, matrix, scale, ct, weighted, tie, chunk, paux, fan, nz, cuts):
    rows, _, naos = blocks.shape
    nscale, width = scale.shape[0], matrix.shape[1]
    piece = jax.ShapeDtypeStruct((nz, width // cuts, width), BF16)

    def whole(shape):
        return pl.BlockSpec(shape, lambda s, *_: (0,) * len(shape))

    return pl.pallas_call(
        functools.partial(rot_kernel, paux, fan, nz, cuts),
        grid_spec=pltpu.PrefetchScalarGridSpec(
            num_scalar_prefetch=1,
            grid=(nscale,),
            in_specs=block_specs(rows, nscale, paux, naos, width, chunk)
            + [whole(ct.shape), whole(weighted.shape), pl.BlockSpec(memory_space=pl.ANY)],
            out_specs=[whole(piece.shape)] * fan + [whole((paux, 1, width))],
            scratch_shapes=[pltpu.VMEM((width // LANES, rows * paux, LANES), F32)],
        ),
        out_shape=[piece] * fan + [jax.ShapeDtypeStruct((paux, 1, width), F32)],
        compiler_params=pltpu.CompilerParams(vmem_limit_bytes=VMEM_BYTES),
        cost_estimate=cost(2 * rows * paux * naos * width, 2 * rows * paux * naos),
    )(me, blocks, matrix, scale, ct, weighted, tie)


def occ_part(blocks, matrix, scale, tie, chunk, paux):
    rows, _, naos = blocks.shape
    nscale, width = scale.shape[0], matrix.shape[1]
    return pl.pallas_call(
        functools.partial(occ_kernel, paux),
        grid=(nscale,),
        in_specs=block_specs(rows, nscale, paux, naos, width, chunk)
        + [pl.BlockSpec(memory_space=pl.ANY)],
        out_specs=pl.BlockSpec((paux, rows, width), lambda s: (0, 0, 0)),
        out_shape=jax.ShapeDtypeStruct((paux, rows, width), BF16),
        scratch_shapes=[pltpu.VMEM((width // LANES, rows * paux, LANES), F32)],
        compiler_params=pltpu.CompilerParams(vmem_limit_bytes=VMEM_BYTES),
        cost_estimate=cost(2 * rows * paux * naos * width, 2 * rows * paux * naos),
    )(blocks, matrix, scale, tie)


def sigma_part(gamma, base, h_occ, ymo):
    paux, width, _ = ymo.shape
    rows = h_occ.shape[1]
    batch = 4 if paux % 4 == 0 else 1
    total = pl.BlockSpec((rows, width), lambda s: (0, 0))
    return pl.pallas_call(
        functools.partial(sigma_kernel, batch),
        grid=(paux // batch,),
        in_specs=[
            pl.BlockSpec(memory_space=pltpu.SMEM),
            total,
            pl.BlockSpec((batch, rows, width), lambda s: (s, 0, 0)),
            pl.BlockSpec((batch, width, width), lambda s: (s, 0, 0)),
        ],
        out_specs=total,
        out_shape=jax.ShapeDtypeStruct((rows, width), F32),
        compiler_params=pltpu.CompilerParams(vmem_limit_bytes=VMEM_BYTES),
        cost_estimate=cost(2 * rows * paux * width * width, 2 * paux * width * width),
    )(gamma, base, h_occ, ymo)


def after(value, others):
    return lax.optimization_barrier((value, others))[0]


def body(blocks, block_scale, coeff, rot_coeff, occupation):
    groups, parts = lax.axis_size("ao"), lax.axis_size("aux")
    nz, nx, ncore = layout_of(groups)
    fan = nx * ncore
    naux, rows, naos = blocks.shape
    nint = coeff.shape[1]
    width = up_to(nint, LANES)
    index = lax.axis_index("ao")
    z = index // fan
    me = jnp.reshape(index % fan, (1,)).astype(jnp.int32)

    def swap(value, bit):
        return lax.ppermute(value, "ao", [(i, i ^ bit) for i in range(groups)])

    def turn_z(value, by):
        return lax.ppermute(value, "ao", [(i, (i + by * fan) % groups) for i in range(groups)])

    def pick(value, k):
        return lax.dynamic_index_in_dim(value, k % nz, 0, keepdims=False)

    def gathered(local):
        wide = jnp.pad(local, ((0, 0), (0, width - nint)))
        return lax.all_gather(wide, "ao", axis=0, tiled=True)

    paux = 8 if naux % 8 == 0 else naux
    chunks = naux // paux
    cuts = groups // paux

    by_rows = blocks.transpose(1, 0, 2)
    scale = block_scale.T[:, :, None]
    ct = jnp.pad(coeff.T, ((0, width - nint), (0, 0))).reshape(cuts, width // cuts, rows)
    ct = jnp.concatenate(
        [lax.dynamic_index_in_dim(ct, index % cuts ^ e, 0, keepdims=False) for e in range(cuts)]
    )
    weighted = jnp.pad(coeff.astype(F32) * occupation[None, :], ((0, 0), (0, width - nint)))
    whole_r = gathered(rot_coeff)
    whole_c = gathered(coeff)
    bits = [1 << k for k in range(fan.bit_length() - 1)]

    def reduce_steps(first):
        live = dict(enumerate(first))
        for bit in bits:
            sent = {d: swap(v, bit) for d, v in live.items() if d & bit}
            sent = yield sent, list(live.values())
            live = {d: v + sent[d | bit] for d, v in live.items() if not d & bit}
        mine = live[0]
        got = [turn_z(pick(mine, z + d), d) for d in range(1, nz)]
        got = yield got, mine
        total = pick(mine, z).astype(F32)
        for part in got:
            total = total + part.astype(F32)
        shard_sum = total.astype(BF16)
        whole = lax.all_gather(shard_sum, "ao", axis=0, tiled=True)
        yield whole.reshape(paux, width, width), shard_sum

    flows, waiting, occ, gammas = [], [], [], []
    start = jnp.zeros((8, LANES), F32)

    def in_transit(c):
        return not isinstance(waiting[c], jax.Array)

    def advance(which, done=()):
        which = [c for c in which if in_transit(c)]
        arrived = after([waiting[c] for c in which], done)
        for c, got in zip(which, arrived):
            waiting[c], marks[c] = flows[c].send(got)

    marks = {}
    for c in range(chunks):
        *first, g = rot_part(
            me, by_rows, whole_r, scale, ct, weighted, after(start, marks), c, paux, fan, nz, cuts
        )
        gammas.append(g)
        flows.append(reduce_steps(first))
        got, marks[c] = next(flows[c])
        waiting.append(got)
        advance(range(c + 1), g)
    gamma = jnp.sum(jnp.concatenate(gammas, axis=0), axis=(1, 2))
    bit = 1
    for c in range(chunks):
        got = swap(gamma, bit) if bit < groups else None
        out = occ_part(by_rows, whole_c, scale, after(start, (marks, gamma)), c, paux)
        occ.append(out)
        if got is not None:
            gamma = gamma + after(got, out)
            bit *= 2
        if any(in_transit(e) for e in range(chunks)):
            advance(range(chunks), out)
    while any(in_transit(e) for e in range(chunks)):
        advance(range(chunks))
    while bit < groups:
        gamma = gamma + swap(gamma, bit)
        bit *= 2

    sigma = jnp.zeros((rows, width), F32)
    for c in range(chunks):
        sigma = sigma_part(gamma[c * paux : (c + 1) * paux], sigma, occ[c], waiting[c])
    bit = 1
    while bit < parts:
        sigma = sigma + lax.ppermute(sigma, "aux", [(i, i ^ bit) for i in range(parts)])
        bit *= 2
    return sigma[:, :nint] / math.sqrt(naux * parts * nint)


def solution(mesh):
    in_specs = (P("aux", "ao", None), P("aux", "ao"), P("ao", None), P("ao", None), P())
    out_specs = P("ao", None)
    return jax.shard_map(body, mesh=mesh, in_specs=in_specs, out_specs=out_specs, check_vma=False)
```

```python
import functools
import math

import jax
import jax.numpy as jnp
from jax import lax
from jax.experimental import pallas as pl
from jax.experimental.pallas import tpu as pltpu
from jax.sharding import PartitionSpec as P

BF16, F32 = jnp.bfloat16, jnp.float32
VMEM_BYTES = 50 * 2**20
LANES = 128


def up_to(value, step):
    return -(-value // step) * step


def layout_of(groups):
    core = 2 if groups % 2 == 0 else 1
    chips = groups // core
    x = 1
    while 4 * x * x <= chips and chips % (2 * x) == 0:
        x *= 2
    return chips // x, x, core


def rows_times(b_ref, m_ref, scale_ref, h_ref):
    mub, paux, naos = b_ref.shape
    step = pl.program_id(0)
    h = jnp.dot(b_ref[...].reshape(mub * paux, naos), m_ref[...], preferred_element_type=F32)
    h = h.reshape(mub, paux, -1) * scale_ref[...]
    h = h.reshape(mub * paux, -1).astype(BF16).astype(F32)
    first = pl.multiple_of(step * (mub * paux), 8)
    for t in range(h_ref.shape[0]):
        h_ref[t, pl.ds(first, mub * paux), :] = h[:, t * LANES : (t + 1) * LANES]


def rows_of(h_ref, p, paux):
    rows = h_ref.shape[1] // paux
    return jnp.concatenate(
        [h_ref[t, pl.ds(p, rows, stride=paux), :] for t in range(h_ref.shape[0])], axis=1
    )


def rot_kernel(paux, fan, nz, cuts, me_ref, b_ref, m_ref, scale_ref, ct_ref, w_ref, tie_ref, *rest):
    outs, gamma_ref, h_ref = rest[:fan], rest[fan], rest[fan + 1]
    rows_times(b_ref, m_ref, scale_ref, h_ref)

    @pl.when(pl.program_id(0) == pl.num_programs(0) - 1)
    def _():
        width = ct_ref.shape[0]
        shard = width // cuts
        for d in range(0, fan, cuts):
            wide = []
            for k in range(nz):
                p = (k * fan + jnp.bitwise_xor(me_ref[0], d)) // cuts
                hp = rows_of(h_ref, p, paux)
                gamma_ref[pl.ds(p, 1)] = jnp.sum(hp * w_ref[...], axis=0, keepdims=True)[None]
                wide.append(hp.astype(BF16))
            y = jnp.dot(ct_ref[...], jnp.concatenate(wide, axis=1), preferred_element_type=F32)
            y = y.astype(BF16)
            for k in range(nz):
                for e in range(cuts):
                    outs[d + e][k] = y[e * shard : (e + 1) * shard, k * width : (k + 1) * width]


def occ_kernel(paux, b_ref, m_ref, scale_ref, tie_ref, out_ref, h_ref):
    rows_times(b_ref, m_ref, scale_ref, h_ref)

    @pl.when(pl.program_id(0) == pl.num_programs(0) - 1)
    def _():
        for p in range(paux):
            out_ref[p] = rows_of(h_ref, p, paux).astype(BF16)


def sigma_kernel(batch, gamma_ref, base_ref, h_ref, y_ref, out_ref):
    step = pl.program_id(0)

    @pl.when(step == 0)
    def _():
        out_ref[...] = base_ref[...]

    h = jnp.concatenate([h_ref[b] for b in range(batch)], axis=1)
    y = y_ref[...].reshape(-1, y_ref.shape[2])
    acc = out_ref[...] - jnp.dot(h, y, preferred_element_type=F32)
    for b in range(batch):
        acc = acc + (2.0 * gamma_ref[step * batch + b]) * h_ref[b].astype(F32)
    out_ref[...] = acc


def shards_kernel(count, owners_ref, gamma_ref, base_ref, h_ref, *rest):
    y_refs, out_ref = rest[:count], rest[count]
    batch = 4 if count % 4 == 0 else 1
    acc = base_ref[...]
    for first in range(0, count, batch):
        some = range(first, first + batch)
        h = [h_ref[owners_ref[i]] for i in some]
        y = jnp.concatenate([y_refs[i][...] for i in some], axis=0)
        acc = acc - jnp.dot(jnp.concatenate(h, axis=1), y, preferred_element_type=F32)
        for i, one in zip(some, h):
            acc = acc + (2.0 * gamma_ref[owners_ref[i]]) * one.astype(F32)
    out_ref[...] = acc


def cost(flops, nbytes):
    return pl.CostEstimate(flops=flops, bytes_accessed=nbytes, transcendentals=0)


def block_specs(rows, nscale, paux, naos, width, chunk):
    mub = rows // nscale
    return [
        pl.BlockSpec((mub, paux, naos), lambda s, *_: (s, chunk, 0)),
        pl.BlockSpec((naos, width), lambda s, *_: (0, 0), pipeline_mode=pl.Buffered(1)),
        pl.BlockSpec((1, paux, 1), lambda s, *_: (s, chunk, 0)),
    ]


def rot_part(me, blocks, matrix, scale, ct, weighted, tie, chunk, paux, fan, nz, cuts):
    rows, _, naos = blocks.shape
    nscale, width = scale.shape[0], matrix.shape[1]
    piece = jax.ShapeDtypeStruct((nz, width // cuts, width), BF16)

    def whole(shape):
        return pl.BlockSpec(shape, lambda s, *_: (0,) * len(shape))

    return pl.pallas_call(
        functools.partial(rot_kernel, paux, fan, nz, cuts),
        grid_spec=pltpu.PrefetchScalarGridSpec(
            num_scalar_prefetch=1,
            grid=(nscale,),
            in_specs=block_specs(rows, nscale, paux, naos, width, chunk)
            + [whole(ct.shape), whole(weighted.shape), pl.BlockSpec(memory_space=pl.ANY)],
            out_specs=[whole(piece.shape)] * fan + [whole((paux, 1, width))],
            scratch_shapes=[pltpu.VMEM((width // LANES, rows * paux, LANES), F32)],
        ),
        out_shape=[piece] * fan + [jax.ShapeDtypeStruct((paux, 1, width), F32)],
        compiler_params=pltpu.CompilerParams(vmem_limit_bytes=VMEM_BYTES),
        cost_estimate=cost(2 * rows * paux * naos * width, 2 * rows * paux * naos),
    )(me, blocks, matrix, scale, ct, weighted, tie)


def occ_part(blocks, matrix, scale, tie, chunk, paux):
    rows, _, naos = blocks.shape
    nscale, width = scale.shape[0], matrix.shape[1]
    return pl.pallas_call(
        functools.partial(occ_kernel, paux),
        grid=(nscale,),
        in_specs=block_specs(rows, nscale, paux, naos, width, chunk)
        + [pl.BlockSpec(memory_space=pl.ANY)],
        out_specs=pl.BlockSpec((paux, rows, width), lambda s: (0, 0, 0)),
        out_shape=jax.ShapeDtypeStruct((paux, rows, width), BF16),
        scratch_shapes=[pltpu.VMEM((width // LANES, rows * paux, LANES), F32)],
        compiler_params=pltpu.CompilerParams(vmem_limit_bytes=VMEM_BYTES),
        cost_estimate=cost(2 * rows * paux * naos * width, 2 * rows * paux * naos),
    )(blocks, matrix, scale, tie)


def sigma_part(gamma, base, h_occ, ymo):
    paux, width, _ = ymo.shape
    rows = h_occ.shape[1]
    batch = 4 if paux % 4 == 0 else 1
    total = pl.BlockSpec((rows, width), lambda s: (0, 0))
    return pl.pallas_call(
        functools.partial(sigma_kernel, batch),
        grid=(paux // batch,),
        in_specs=[
            pl.BlockSpec(memory_space=pltpu.SMEM),
            total,
            pl.BlockSpec((batch, rows, width), lambda s: (s, 0, 0)),
            pl.BlockSpec((batch, width, width), lambda s: (s, 0, 0)),
        ],
        out_specs=total,
        out_shape=jax.ShapeDtypeStruct((rows, width), F32),
        compiler_params=pltpu.CompilerParams(vmem_limit_bytes=VMEM_BYTES),
        cost_estimate=cost(2 * rows * paux * width * width, 2 * paux * width * width),
    )(gamma, base, h_occ, ymo)


def sigma_shards(owners, gamma, base, h_occ, shards):
    paux, rows, width = h_occ.shape
    return pl.pallas_call(
        functools.partial(shards_kernel, len(shards)),
        in_specs=[pl.BlockSpec(memory_space=pltpu.SMEM)] * 2
        + [pl.BlockSpec(memory_space=pltpu.VMEM)] * (2 + len(shards)),
        out_specs=pl.BlockSpec(memory_space=pltpu.VMEM),
        out_shape=jax.ShapeDtypeStruct((rows, width), F32),
        compiler_params=pltpu.CompilerParams(vmem_limit_bytes=VMEM_BYTES),
        cost_estimate=cost(2 * rows * len(shards) * width * width, 2 * len(shards) * width * width),
    )(owners, gamma, base, h_occ, *shards)


def after(value, others):
    return lax.optimization_barrier((value, others))[0]


def body(blocks, block_scale, coeff, rot_coeff, occupation):
    groups, parts = lax.axis_size("ao"), lax.axis_size("aux")
    nz, nx, ncore = layout_of(groups)
    fan = nx * ncore
    naux, rows, naos = blocks.shape
    nint = coeff.shape[1]
    width = up_to(nint, LANES)
    index = lax.axis_index("ao")
    z = index // fan
    me = jnp.reshape(index % fan, (1,)).astype(jnp.int32)

    def swap(value, bit):
        return lax.ppermute(value, "ao", [(i, i ^ bit) for i in range(groups)])

    def turn_z(value, by):
        return lax.ppermute(value, "ao", [(i, (i + by * fan) % groups) for i in range(groups)])

    def pick(value, k):
        return lax.dynamic_index_in_dim(value, k % nz, 0, keepdims=False)

    def gathered(local):
        wide = jnp.pad(local, ((0, 0), (0, width - nint)))
        return lax.all_gather(wide, "ao", axis=0, tiled=True)

    paux = 16 if naux % 16 == 0 else naux
    chunks = naux // paux
    cuts = groups // paux

    by_rows = blocks.transpose(1, 0, 2)
    scale = block_scale.T[:, :, None]
    ct = jnp.pad(coeff.T, ((0, width - nint), (0, 0))).reshape(cuts, width // cuts, rows)
    ct = jnp.concatenate(
        [lax.dynamic_index_in_dim(ct, index % cuts ^ e, 0, keepdims=False) for e in range(cuts)]
    )
    weighted = jnp.pad(coeff.astype(F32) * occupation[None, :], ((0, 0), (0, width - nint)))
    whole_r = gathered(rot_coeff)
    whole_c = gathered(coeff)
    bits = [1 << k for k in range(fan.bit_length() - 1)]

    def reduce_steps(first, by_permutes):
        live = dict(enumerate(first))
        for bit in bits:
            sent = {d: swap(v, bit) for d, v in live.items() if d & bit}
            sent = yield sent, list(live.values())
            live = {d: v + sent[d | bit] for d, v in live.items() if not d & bit}
        mine = live[0]
        sent = [pick(mine, z + d) for d in range(1, nz)]
        got = yield [turn_z(v, d + 1) for d, v in enumerate(sent)], sent
        total = pick(mine, z).astype(F32)
        for part in got:
            total = total + part.astype(F32)
        total = total.astype(BF16)
        if not by_permutes:
            whole = lax.all_gather(total, "ao", axis=0, tiled=True)
            yield whole.reshape(paux, width, width), total
            return
        shards = [[total] + [turn_z(total, d) for d in range(1, nz)]]
        for bit in reversed(bits):
            shards = shards + [[swap(v, bit) for v in column] for column in shards]
        yield shards, total

    flows, waiting, occ, gammas = [], [], [], []
    start = jnp.zeros((8, LANES), F32)

    left = [len(bits) + 1] * chunks

    def in_transit(c):
        return left[c] > 0

    def advance(which, done=()):
        which = [c for c in which if in_transit(c)]
        arrived = after([waiting[c] for c in which], done)
        for c, got in zip(which, arrived):
            waiting[c], marks[c] = flows[c].send(got)
            left[c] -= 1

    marks = {}
    for c in range(chunks):
        *first, g = rot_part(
            me, by_rows, whole_r, scale, ct, weighted, after(start, marks), c, paux, fan, nz, cuts
        )
        gammas.append(g)
        flows.append(reduce_steps(first, cuts == 1 and c == chunks - 1 > 0))
        got, marks[c] = next(flows[c])
        waiting.append(got)
        advance(range(c + 1), g)
    gamma = jnp.sum(jnp.concatenate(gammas, axis=0), axis=(1, 2))
    bit = 1
    for c in range(chunks):
        got = swap(gamma, bit) if bit < groups else None
        out = occ_part(by_rows, whole_c, scale, after(start, (marks, gamma)), c, paux)
        occ.append(out)
        if got is not None:
            gamma = gamma + after(got, out)
            bit *= 2
        if any(left):
            advance(range(chunks), out)
    while any(left):
        advance(range(chunks))
    while bit < groups:
        gamma = gamma + swap(gamma, bit)
        bit *= 2

    sigma = jnp.zeros((rows, width), F32)
    for c in range(chunks):
        g = gamma[c * paux : (c + 1) * paux]
        if isinstance(waiting[c], jax.Array):
            sigma = sigma_part(g, sigma, occ[c], waiting[c])
            continue
        shards = waiting[c]
        order = [0]
        for bit in reversed(bits):
            order = order + [d ^ bit for d in order]
        for lo in range(0, fan, fan // ncore):
            some = range(lo, lo + fan // ncore)
            owners = [(z - k) % nz * fan + (index % fan ^ order[d]) for d in some for k in range(nz)]
            sigma = sigma_shards(
                jnp.stack(owners).astype(jnp.int32), g, sigma, occ[c], [v for d in some for v in shards[d]]
            )
    bit = 1
    while bit < parts:
        sigma = sigma + lax.ppermute(sigma, "aux", [(i, i ^ bit) for i in range(parts)])
        bit *= 2
    return sigma[:, :nint] / math.sqrt(naux * parts * nint)


def solution(mesh):
    in_specs = (P("aux", "ao", None), P("aux", "ao"), P("ao", None), P("ao", None), P())
    out_specs = P("ao", None)
    return jax.shard_map(body, mesh=mesh, in_specs=in_specs, out_specs=out_specs, check_vma=False)
```

```python
import functools
import math

import jax
import jax.numpy as jnp
from jax import lax
from jax.experimental import pallas as pl
from jax.experimental.pallas import tpu as pltpu
from jax.sharding import PartitionSpec as P

BF16, F32 = jnp.bfloat16, jnp.float32
VMEM_BYTES = 50 * 2**20
LANES = 128


def up_to(value, step):
    return -(-value // step) * step


def layout_of(groups):
    core = 2 if groups % 2 == 0 else 1
    chips = groups // core
    x = 1
    while 4 * x * x <= chips and chips % (2 * x) == 0:
        x *= 2
    return chips // x, x, core


def joined(parts_ref, m_ref):
    count, rows, cols = parts_ref.shape
    if cols < m_ref.shape[1]:
        m_ref[:, cols - cols % LANES :] = jnp.zeros((m_ref.shape[0], LANES), BF16)
    for k in range(count):
        m_ref[k * rows : (k + 1) * rows, :cols] = parts_ref[k]


def rows_times(b_ref, m_ref, scale_ref, h_ref):
    mub, paux, naos = b_ref.shape
    step = pl.program_id(0)
    h = jnp.dot(b_ref[...].reshape(mub * paux, naos), m_ref[...], preferred_element_type=F32)
    h = h.reshape(mub, paux, -1) * scale_ref[...]
    h = h.reshape(mub * paux, -1).astype(BF16).astype(F32)
    first = pl.multiple_of(step * (mub * paux), 8)
    for t in range(h_ref.shape[0]):
        h_ref[t, pl.ds(first, mub * paux), :] = h[:, t * LANES : (t + 1) * LANES]


def rows_of(h_ref, p, paux):
    rows = h_ref.shape[1] // paux
    return jnp.concatenate(
        [h_ref[t, pl.ds(p, rows, stride=paux), :] for t in range(h_ref.shape[0])], axis=1
    )


def rot_kernel(paux, fan, nz, cuts, me_ref, b_ref, m_ref, scale_ref, ct_ref, w_ref, tie_ref, *rest):
    outs, gamma_ref, h_ref = rest[:fan], rest[fan], rest[-1]
    if len(m_ref.shape) == 3:
        parts_ref, m_ref = m_ref, rest[fan + 1]
        pl.when(pl.program_id(0) == 0)(lambda: joined(parts_ref, m_ref))
    rows_times(b_ref, m_ref, scale_ref, h_ref)

    @pl.when(pl.program_id(0) == pl.num_programs(0) - 1)
    def _():
        width = ct_ref.shape[0]
        shard = width // cuts
        for d in range(0, fan, cuts):
            wide = []
            for k in range(nz):
                p = (k * fan + jnp.bitwise_xor(me_ref[0], d)) // cuts
                hp = rows_of(h_ref, p, paux)
                gamma_ref[pl.ds(p, 1)] = jnp.sum(hp * w_ref[...], axis=0, keepdims=True)[None]
                wide.append(hp.astype(BF16))
            y = jnp.dot(ct_ref[...], jnp.concatenate(wide, axis=1), preferred_element_type=F32)
            y = y.astype(BF16)
            for k in range(nz):
                for e in range(cuts):
                    outs[d + e][k] = y[e * shard : (e + 1) * shard, k * width : (k + 1) * width]


def occ_kernel(paux, b_ref, m_ref, scale_ref, tie_ref, out_ref, *rest):
    h_ref = rest[-1]
    if len(m_ref.shape) == 3:
        parts_ref, m_ref = m_ref, rest[0]
        pl.when(pl.program_id(0) == 0)(lambda: joined(parts_ref, m_ref))
    rows_times(b_ref, m_ref, scale_ref, h_ref)

    @pl.when(pl.program_id(0) == pl.num_programs(0) - 1)
    def _():
        for p in range(paux):
            out_ref[p] = rows_of(h_ref, p, paux).astype(BF16)


def sigma_kernel(batch, gamma_ref, base_ref, h_ref, y_ref, out_ref):
    step = pl.program_id(0)

    @pl.when(step == 0)
    def _():
        out_ref[...] = base_ref[...]

    h = jnp.concatenate([h_ref[b] for b in range(batch)], axis=1)
    y = y_ref[...].reshape(-1, y_ref.shape[2])
    acc = out_ref[...] - jnp.dot(h, y, preferred_element_type=F32)
    for b in range(batch):
        acc = acc + (2.0 * gamma_ref[step * batch + b]) * h_ref[b].astype(F32)
    out_ref[...] = acc


def shards_kernel(count, owners_ref, gamma_ref, base_ref, h_ref, *rest):
    y_refs, out_ref = rest[:count], rest[count]
    batch = 4 if count % 4 == 0 else 1
    acc = base_ref[...]
    for first in range(0, count, batch):
        some = range(first, first + batch)
        h = [h_ref[owners_ref[i]] for i in some]
        y = jnp.concatenate([y_refs[i][...] for i in some], axis=0)
        acc = acc - jnp.dot(jnp.concatenate(h, axis=1), y, preferred_element_type=F32)
        for i, one in zip(some, h):
            acc = acc + (2.0 * gamma_ref[owners_ref[i]]) * one.astype(F32)
    out_ref[...] = acc


def cost(flops, nbytes):
    return pl.CostEstimate(flops=flops, bytes_accessed=nbytes, transcendentals=0)


def block_specs(rows, nscale, paux, naos, shape, chunk):
    mub = rows // nscale
    return [
        pl.BlockSpec((mub, paux, naos), lambda s, *_: (s, chunk, 0)),
        pl.BlockSpec(shape, lambda s, *_: (0,) * len(shape), pipeline_mode=pl.Buffered(1)),
        pl.BlockSpec((1, paux, 1), lambda s, *_: (s, chunk, 0)),
    ]


def rot_part(me, blocks, matrix, scale, ct, weighted, tie, chunk, paux, fan, nz, cuts):
    rows, _, naos = blocks.shape
    nscale, width = scale.shape[0], up_to(matrix.shape[-1], LANES)
    extra = [(naos, width)] if matrix.ndim == 3 else []
    piece = jax.ShapeDtypeStruct((nz, width // cuts, width), BF16)

    def whole(shape):
        return pl.BlockSpec(shape, lambda s, *_: (0,) * len(shape))

    return pl.pallas_call(
        functools.partial(rot_kernel, paux, fan, nz, cuts),
        grid_spec=pltpu.PrefetchScalarGridSpec(
            num_scalar_prefetch=1,
            grid=(nscale,),
            in_specs=block_specs(rows, nscale, paux, naos, matrix.shape, chunk)
            + [whole(ct.shape), whole(weighted.shape), pl.BlockSpec(memory_space=pl.ANY)],
            out_specs=[whole(piece.shape)] * fan
            + [whole((paux, 1, width))]
            + [pl.BlockSpec(e, lambda s, *_: (0, 0)) for e in extra],
            scratch_shapes=[pltpu.VMEM((width // LANES, rows * paux, LANES), F32)],
        ),
        out_shape=[piece] * fan
        + [jax.ShapeDtypeStruct((paux, 1, width), F32)]
        + [jax.ShapeDtypeStruct(e, BF16) for e in extra],
        compiler_params=pltpu.CompilerParams(vmem_limit_bytes=VMEM_BYTES),
        cost_estimate=cost(2 * rows * paux * naos * width, 2 * rows * paux * naos),
    )(me, blocks, matrix, scale, ct, weighted, tie)


def occ_part(blocks, matrix, scale, tie, chunk, paux):
    rows, _, naos = blocks.shape
    nscale, width = scale.shape[0], up_to(matrix.shape[-1], LANES)
    extra = [(naos, width)] if matrix.ndim == 3 else []
    out = jax.ShapeDtypeStruct((paux, rows, width), BF16)
    return pl.pallas_call(
        functools.partial(occ_kernel, paux),
        grid=(nscale,),
        in_specs=block_specs(rows, nscale, paux, naos, matrix.shape, chunk)
        + [pl.BlockSpec(memory_space=pl.ANY)],
        out_specs=[pl.BlockSpec(out.shape, lambda s: (0, 0, 0))]
        + [pl.BlockSpec(e, lambda s: (0, 0)) for e in extra],
        out_shape=[out] + [jax.ShapeDtypeStruct(e, BF16) for e in extra],
        scratch_shapes=[pltpu.VMEM((width // LANES, rows * paux, LANES), F32)],
        compiler_params=pltpu.CompilerParams(vmem_limit_bytes=VMEM_BYTES),
        cost_estimate=cost(2 * rows * paux * naos * width, 2 * rows * paux * naos),
    )(blocks, matrix, scale, tie)


def sigma_part(gamma, base, h_occ, ymo):
    paux, width, _ = ymo.shape
    rows = h_occ.shape[1]
    batch = 4 if paux % 4 == 0 else 1
    total = pl.BlockSpec((rows, width), lambda s: (0, 0))
    return pl.pallas_call(
        functools.partial(sigma_kernel, batch),
        grid=(paux // batch,),
        in_specs=[
            pl.BlockSpec(memory_space=pltpu.SMEM),
            total,
            pl.BlockSpec((batch, rows, width), lambda s: (s, 0, 0)),
            pl.BlockSpec((batch, width, width), lambda s: (s, 0, 0)),
        ],
        out_specs=total,
        out_shape=jax.ShapeDtypeStruct((rows, width), F32),
        compiler_params=pltpu.CompilerParams(vmem_limit_bytes=VMEM_BYTES),
        cost_estimate=cost(2 * rows * paux * width * width, 2 * paux * width * width),
    )(gamma, base, h_occ, ymo)


def sigma_shards(owners, gamma, base, h_occ, shards):
    paux, rows, width = h_occ.shape
    return pl.pallas_call(
        functools.partial(shards_kernel, len(shards)),
        in_specs=[pl.BlockSpec(memory_space=pltpu.SMEM)] * 2
        + [pl.BlockSpec(memory_space=pltpu.VMEM)] * (2 + len(shards)),
        out_specs=pl.BlockSpec(memory_space=pltpu.VMEM),
        out_shape=jax.ShapeDtypeStruct((rows, width), F32),
        compiler_params=pltpu.CompilerParams(vmem_limit_bytes=VMEM_BYTES),
        cost_estimate=cost(2 * rows * len(shards) * width * width, 2 * len(shards) * width * width),
    )(owners, gamma, base, h_occ, *shards)


def after(value, others):
    return lax.optimization_barrier((value, others))[0]


def body(blocks, block_scale, coeff, rot_coeff, occupation):
    groups, parts = lax.axis_size("ao"), lax.axis_size("aux")
    nz, nx, ncore = layout_of(groups)
    fan = nx * ncore
    naux, rows, naos = blocks.shape
    nint = coeff.shape[1]
    width = up_to(nint, LANES)
    index = lax.axis_index("ao")
    z = index // fan
    me = jnp.reshape(index % fan, (1,)).astype(jnp.int32)

    def swap(value, bit):
        return lax.ppermute(value, "ao", [(i, i ^ bit) for i in range(groups)])

    def turn_z(value, by):
        return lax.ppermute(value, "ao", [(i, (i + by * fan) % groups) for i in range(groups)])

    def pick(value, k):
        return lax.dynamic_index_in_dim(value, k % nz, 0, keepdims=False)

    paux = 16 if naux % 16 == 0 else naux
    chunks = naux // paux
    cuts = groups // paux

    by_rows = blocks.transpose(1, 0, 2)
    scale = block_scale.T[:, :, None]
    ct = jnp.pad(coeff.T, ((0, width - nint), (0, 0))).reshape(cuts, width // cuts, rows)
    ct = jnp.concatenate(
        [lax.dynamic_index_in_dim(ct, index % cuts ^ e, 0, keepdims=False) for e in range(cuts)]
    )
    weighted = jnp.pad(coeff.astype(F32) * occupation[None, :], ((0, 0), (0, width - nint)))
    whole_r = lax.all_gather(rot_coeff, "ao", axis=0)
    whole_c = lax.all_gather(coeff, "ao", axis=0)
    bits = [1 << k for k in range(fan.bit_length() - 1)]

    def reduce_steps(first, by_permutes):
        live = dict(enumerate(first))
        for bit in bits:
            sent = {d: swap(v, bit) for d, v in live.items() if d & bit}
            sent = yield sent, list(live.values())
            live = {d: v + sent[d | bit] for d, v in live.items() if not d & bit}
        mine = live[0]
        sent = [pick(mine, z + d) for d in range(1, nz)]
        got = yield [turn_z(v, d + 1) for d, v in enumerate(sent)], sent
        total = pick(mine, z).astype(F32)
        for part in got:
            total = total + part.astype(F32)
        total = total.astype(BF16)
        if not by_permutes:
            whole = lax.all_gather(total, "ao", axis=0, tiled=True)
            yield whole.reshape(paux, width, width), total
            return
        shards = [[total] + [turn_z(total, d) for d in range(1, nz)]]
        for bit in reversed(bits):
            shards = shards + [[swap(v, bit) for v in column] for column in shards]
        yield shards, total

    flows, waiting, occ, gammas = [], [], [], []
    start = jnp.zeros((8, LANES), F32)

    left = [len(bits) + 1] * chunks

    def in_transit(c):
        return left[c] > 0

    def advance(which, done=()):
        which = [c for c in which if in_transit(c)]
        arrived = after([waiting[c] for c in which], done)
        for c, got in zip(which, arrived):
            waiting[c], marks[c] = flows[c].send(got)
            left[c] -= 1

    marks = {}
    for c in range(chunks):
        out = rot_part(
            me, by_rows, whole_r, scale, ct, weighted, after(start, marks), c, paux, fan, nz, cuts
        )
        first, g = out[:fan], out[fan]
        if c == 0:
            whole_r = out[fan + 1]
        gammas.append(g)
        flows.append(reduce_steps(first, cuts == 1 and c == chunks - 1 > 0))
        got, marks[c] = next(flows[c])
        waiting.append(got)
        advance(range(c + 1), g)
    gamma = jnp.sum(jnp.concatenate(gammas, axis=0), axis=(1, 2))
    hops = [
        [functools.partial(swap, bit=d) for d in range(1, fan)],
        [functools.partial(turn_z, by=d) for d in range(1, nz)],
    ]
    for c in range(chunks):
        hop = hops.pop(0) if hops else []
        got = [move(gamma) for move in hop]
        out, *extra = occ_part(by_rows, whole_c, scale, after(start, (marks, gamma)), c, paux)
        if extra:
            whole_c = extra[0]
        occ.append(out)
        for part in after(got, out):
            gamma = gamma + part
        if any(left):
            advance(range(chunks), (out, gamma))
    for hop in hops:
        gamma = functools.reduce(jnp.add, [move(gamma) for move in hop], gamma)
    while any(left):
        advance(range(chunks))

    sigma = jnp.zeros((rows, width), F32)
    for c in range(chunks):
        g = gamma[c * paux : (c + 1) * paux]
        if isinstance(waiting[c], jax.Array):
            sigma = sigma_part(g, sigma, occ[c], waiting[c])
            continue
        shards = waiting[c]
        order = [0]
        for bit in reversed(bits):
            order = order + [d ^ bit for d in order]
        for lo in range(0, fan, fan // ncore):
            some = range(lo, lo + fan // ncore)
            owners = [(z - k) % nz * fan + (index % fan ^ order[d]) for d in some for k in range(nz)]
            sigma = sigma_shards(
                jnp.stack(owners).astype(jnp.int32), g, sigma, occ[c], [v for d in some for v in shards[d]]
            )
    bit = 1
    while bit < parts:
        sigma = sigma + lax.ppermute(sigma, "aux", [(i, i ^ bit) for i in range(parts)])
        bit *= 2
    return sigma[:, :nint] / math.sqrt(naux * parts * nint)


def solution(mesh):
    in_specs = (P("aux", "ao", None), P("aux", "ao"), P("ao", None), P("ao", None), P())
    out_specs = P("ao", None)
    return jax.shard_map(body, mesh=mesh, in_specs=in_specs, out_specs=out_specs, check_vma=False)
```

```python
import functools
import math

import jax
import jax.numpy as jnp
from jax import lax
from jax.experimental import pallas as pl
from jax.experimental.pallas import tpu as pltpu
from jax.sharding import PartitionSpec as P

BF16, F32 = jnp.bfloat16, jnp.float32
VMEM_BYTES = 50 * 2**20
LANES = 128


def up_to(value, step):
    return -(-value // step) * step


def layout_of(groups):
    core = 2 if groups % 2 == 0 else 1
    chips = groups // core
    x = 1
    while 4 * x * x <= chips and chips % (2 * x) == 0:
        x *= 2
    return chips // x, x, core


def joined(parts_ref, m_ref):
    count, rows, cols = parts_ref.shape
    if cols < m_ref.shape[1]:
        m_ref[:, cols - cols % LANES :] = jnp.zeros((m_ref.shape[0], LANES), BF16)
    for k in range(count):
        m_ref[k * rows : (k + 1) * rows, :cols] = parts_ref[k]


def rows_times(b_ref, m_ref, scale_ref, h_ref):
    mub, paux, naos = b_ref.shape
    step = pl.program_id(0)
    h = jnp.dot(b_ref[...].reshape(mub * paux, naos), m_ref[...], preferred_element_type=F32)
    h = h.reshape(mub, paux, -1) * scale_ref[...]
    h = h.reshape(mub * paux, -1).astype(BF16).astype(F32)
    first = pl.multiple_of(step * (mub * paux), 8)
    for t in range(h_ref.shape[0]):
        h_ref[t, pl.ds(first, mub * paux), :] = h[:, t * LANES : (t + 1) * LANES]


def rows_of(h_ref, p, paux):
    rows = h_ref.shape[1] // paux
    return jnp.concatenate(
        [h_ref[t, pl.ds(p, rows, stride=paux), :] for t in range(h_ref.shape[0])], axis=1
    )


def rot_kernel(paux, fan, nz, cuts, me_ref, b_ref, m_ref, scale_ref, ct_ref, w_ref, tie_ref, *rest):
    outs, gamma_ref, h_ref = rest[:fan], rest[fan], rest[-1]
    if len(m_ref.shape) == 3:
        parts_ref, m_ref = m_ref, rest[fan + 1]
        pl.when(pl.program_id(0) == 0)(lambda: joined(parts_ref, m_ref))
    rows_times(b_ref, m_ref, scale_ref, h_ref)

    @pl.when(pl.program_id(0) == pl.num_programs(0) - 1)
    def _():
        width = ct_ref.shape[0]
        shard = width // cuts
        for d in range(0, fan, cuts):
            wide = []
            for k in range(nz):
                p = (k * fan + jnp.bitwise_xor(me_ref[0], d)) // cuts
                hp = rows_of(h_ref, p, paux)
                gamma_ref[pl.ds(p, 1)] = jnp.sum(hp * w_ref[...], axis=0, keepdims=True)[None]
                wide.append(hp.astype(BF16))
            y = jnp.dot(ct_ref[...], jnp.concatenate(wide, axis=1), preferred_element_type=F32)
            y = y.astype(BF16)
            for k in range(nz):
                for e in range(cuts):
                    outs[d + e][k] = y[e * shard : (e + 1) * shard, k * width : (k + 1) * width]


def occ_kernel(paux, b_ref, m_ref, scale_ref, tie_ref, out_ref, *rest):
    h_ref = rest[-1]
    if len(m_ref.shape) == 3:
        parts_ref, m_ref = m_ref, rest[0]
        pl.when(pl.program_id(0) == 0)(lambda: joined(parts_ref, m_ref))
    rows_times(b_ref, m_ref, scale_ref, h_ref)

    @pl.when(pl.program_id(0) == pl.num_programs(0) - 1)
    def _():
        for p in range(paux):
            out_ref[p] = rows_of(h_ref, p, paux).astype(BF16)


def sigma_kernel(batch, gamma_ref, base_ref, h_ref, y_ref, out_ref):
    step = pl.program_id(0)

    @pl.when(step == 0)
    def _():
        out_ref[...] = base_ref[...]

    h = jnp.concatenate([h_ref[b] for b in range(batch)], axis=1)
    y = y_ref[...].reshape(-1, y_ref.shape[2])
    acc = out_ref[...] - jnp.dot(h, y, preferred_element_type=F32)
    for b in range(batch):
        acc = acc + (2.0 * gamma_ref[step * batch + b]) * h_ref[b].astype(F32)
    out_ref[...] = acc


def shards_kernel(count, owners_ref, gamma_ref, base_ref, h_ref, *rest):
    y_refs, out_ref = rest[:count], rest[count]
    batch = 4 if count % 4 == 0 else 1
    acc = base_ref[...]
    for first in range(0, count, batch):
        some = range(first, first + batch)
        h = [h_ref[owners_ref[i]] for i in some]
        y = jnp.concatenate([y_refs[i][...] for i in some], axis=0)
        acc = acc - jnp.dot(jnp.concatenate(h, axis=1), y, preferred_element_type=F32)
        for i, one in zip(some, h):
            acc = acc + (2.0 * gamma_ref[owners_ref[i]]) * one.astype(F32)
    out_ref[...] = acc


def cost(flops, nbytes):
    return pl.CostEstimate(flops=flops, bytes_accessed=nbytes, transcendentals=0)


def block_specs(rows, nscale, paux, naos, shape, chunk):
    mub = rows // nscale
    return [
        pl.BlockSpec((mub, paux, naos), lambda s, *_: (s, chunk, 0)),
        pl.BlockSpec(shape, lambda s, *_: (0,) * len(shape), pipeline_mode=pl.Buffered(1)),
        pl.BlockSpec((1, paux, 1), lambda s, *_: (s, chunk, 0)),
    ]


def rot_part(me, blocks, matrix, scale, ct, weighted, tie, chunk, paux, fan, nz, cuts):
    rows, _, naos = blocks.shape
    nscale, width = scale.shape[0], up_to(matrix.shape[-1], LANES)
    extra = [(naos, width)] if matrix.ndim == 3 else []
    piece = jax.ShapeDtypeStruct((nz, width // cuts, width), BF16)

    def whole(shape):
        return pl.BlockSpec(shape, lambda s, *_: (0,) * len(shape))

    return pl.pallas_call(
        functools.partial(rot_kernel, paux, fan, nz, cuts),
        grid_spec=pltpu.PrefetchScalarGridSpec(
            num_scalar_prefetch=1,
            grid=(nscale,),
            in_specs=block_specs(rows, nscale, paux, naos, matrix.shape, chunk)
            + [whole(ct.shape), whole(weighted.shape), pl.BlockSpec(memory_space=pl.ANY)],
            out_specs=[whole(piece.shape)] * fan
            + [whole((paux, 1, width))]
            + [pl.BlockSpec(e, lambda s, *_: (0, 0)) for e in extra],
            scratch_shapes=[pltpu.VMEM((width // LANES, rows * paux, LANES), F32)],
        ),
        out_shape=[piece] * fan
        + [jax.ShapeDtypeStruct((paux, 1, width), F32)]
        + [jax.ShapeDtypeStruct(e, BF16) for e in extra],
        compiler_params=pltpu.CompilerParams(vmem_limit_bytes=VMEM_BYTES),
        cost_estimate=cost(2 * rows * paux * naos * width, 2 * rows * paux * naos),
    )(me, blocks, matrix, scale, ct, weighted, tie)


def occ_part(blocks, matrix, scale, tie, chunk, paux):
    rows, _, naos = blocks.shape
    nscale, width = scale.shape[0], up_to(matrix.shape[-1], LANES)
    extra = [(naos, width)] if matrix.ndim == 3 else []
    out = jax.ShapeDtypeStruct((paux, rows, width), BF16)
    return pl.pallas_call(
        functools.partial(occ_kernel, paux),
        grid=(nscale,),
        in_specs=block_specs(rows, nscale, paux, naos, matrix.shape, chunk)
        + [pl.BlockSpec(memory_space=pl.ANY)],
        out_specs=[pl.BlockSpec(out.shape, lambda s: (0, 0, 0))]
        + [pl.BlockSpec(e, lambda s: (0, 0)) for e in extra],
        out_shape=[out] + [jax.ShapeDtypeStruct(e, BF16) for e in extra],
        scratch_shapes=[pltpu.VMEM((width // LANES, rows * paux, LANES), F32)],
        compiler_params=pltpu.CompilerParams(vmem_limit_bytes=VMEM_BYTES),
        cost_estimate=cost(2 * rows * paux * naos * width, 2 * rows * paux * naos),
    )(blocks, matrix, scale, tie)


def sigma_part(gamma, base, h_occ, ymo):
    paux, width, _ = ymo.shape
    rows = h_occ.shape[1]
    batch = 4 if paux % 4 == 0 else 1
    total = pl.BlockSpec((rows, width), lambda s: (0, 0))
    return pl.pallas_call(
        functools.partial(sigma_kernel, batch),
        grid=(paux // batch,),
        in_specs=[
            pl.BlockSpec(memory_space=pltpu.SMEM),
            total,
            pl.BlockSpec((batch, rows, width), lambda s: (s, 0, 0)),
            pl.BlockSpec((batch, width, width), lambda s: (s, 0, 0)),
        ],
        out_specs=total,
        out_shape=jax.ShapeDtypeStruct((rows, width), F32),
        compiler_params=pltpu.CompilerParams(vmem_limit_bytes=VMEM_BYTES),
        cost_estimate=cost(2 * rows * paux * width * width, 2 * paux * width * width),
    )(gamma, base, h_occ, ymo)


def sigma_shards(owners, gamma, base, h_occ, shards):
    paux, rows, width = h_occ.shape
    return pl.pallas_call(
        functools.partial(shards_kernel, len(shards)),
        in_specs=[pl.BlockSpec(memory_space=pltpu.SMEM)] * 2
        + [pl.BlockSpec(memory_space=pltpu.VMEM)] * (2 + len(shards)),
        out_specs=pl.BlockSpec(memory_space=pltpu.VMEM),
        out_shape=jax.ShapeDtypeStruct((rows, width), F32),
        compiler_params=pltpu.CompilerParams(vmem_limit_bytes=VMEM_BYTES),
        cost_estimate=cost(2 * rows * len(shards) * width * width, 2 * len(shards) * width * width),
    )(owners, gamma, base, h_occ, *shards)


def after(value, others):
    return lax.optimization_barrier((value, others))[0]


def body(blocks, block_scale, coeff, rot_coeff, occupation):
    groups, parts = lax.axis_size("ao"), lax.axis_size("aux")
    nz, nx, ncore = layout_of(groups)
    fan = nx * ncore
    naux, rows, naos = blocks.shape
    nint = coeff.shape[1]
    width = up_to(nint, LANES)
    index = lax.axis_index("ao")
    z = index // fan
    me = jnp.reshape(index % fan, (1,)).astype(jnp.int32)

    def swap(value, bit):
        return lax.ppermute(value, "ao", [(i, i ^ bit) for i in range(groups)])

    def turn_z(value, by):
        return lax.ppermute(value, "ao", [(i, (i + by * fan) % groups) for i in range(groups)])

    def pick(value, k):
        return lax.dynamic_index_in_dim(value, k % nz, 0, keepdims=False)

    paux = 16 if naux % 16 == 0 else naux
    chunks = naux // paux
    cuts = groups // paux

    by_rows = blocks.transpose(1, 0, 2)
    scale = block_scale.T[:, :, None]
    ct = jnp.pad(coeff.T, ((0, width - nint), (0, 0))).reshape(cuts, width // cuts, rows)
    ct = jnp.concatenate(
        [lax.dynamic_index_in_dim(ct, index % cuts ^ e, 0, keepdims=False) for e in range(cuts)]
    )
    weighted = jnp.pad(coeff.astype(F32) * occupation[None, :], ((0, 0), (0, width - nint)))
    whole_r = lax.all_gather(rot_coeff, "ao", axis=0)
    whole_c = lax.all_gather(coeff, "ao", axis=0)
    bits = [1 << k for k in range(fan.bit_length() - 1)]

    def reduce_steps(first, by_permutes):
        live = dict(enumerate(first))
        for bit in bits:
            sent = {d: swap(v, bit) for d, v in live.items() if d & bit}
            sent = yield sent, list(live.values())
            live = {d: v + sent[d | bit] for d, v in live.items() if not d & bit}
        mine = live[0]
        sent = [pick(mine, z + d) for d in range(1, nz)]
        got = yield [turn_z(v, d + 1) for d, v in enumerate(sent)], sent
        total = pick(mine, z).astype(F32)
        for part in got:
            total = total + part.astype(F32)
        total = total.astype(BF16)
        if not by_permutes:
            whole = lax.all_gather(total, "ao", axis=0, tiled=True)
            yield whole.reshape(paux, width, width), total
            return
        shards = [[total] + [turn_z(total, d) for d in range(1, nz)]]
        for bit in reversed(bits):
            shards = shards + [[swap(v, bit) for v in column] for column in shards]
        yield shards, total

    flows, waiting, occ, gammas = [], [], [], []
    start = jnp.zeros((8, LANES), F32)

    left = [len(bits) + 1] * chunks

    def in_transit(c):
        return left[c] > 0

    def advance(which, done=(), chained=False):
        which = [c for c in which if in_transit(c)]
        arrived = after([waiting[c] for c in which], done)
        sent = ()
        for c, got in zip(which, arrived):
            waiting[c], marks[c] = flows[c].send(after(got, sent) if chained else got)
            sent = marks[c]
            left[c] -= 1

    marks = {}
    for c in range(chunks):
        out = rot_part(
            me, by_rows, whole_r, scale, ct, weighted, after(start, marks), c, paux, fan, nz, cuts
        )
        first, g = after(out[:fan], waiting), out[fan]
        if c == 0:
            whole_r = out[fan + 1]
        gammas.append(g)
        flows.append(reduce_steps(first, cuts == 1 and c == chunks - 1 > 0))
        got, marks[c] = next(flows[c])
        waiting.append(got)
        advance(range(c + 1), g, chained=True)
    gamma = jnp.sum(jnp.concatenate(gammas, axis=0), axis=(1, 2))
    gamma = functools.reduce(jnp.add, [swap(gamma, d) for d in range(1, fan)], gamma)
    far = [turn_z(gamma, d) for d in range(1, nz)]
    for c in range(chunks):
        out, *extra = occ_part(by_rows, whole_c, scale, after(start, (marks, gamma)), c, paux)
        if extra:
            whole_c = extra[0]
        occ.append(out)
        if c == 0:
            gamma = functools.reduce(jnp.add, after(far, out), gamma)
        if any(left):
            advance(reversed(range(chunks)), (out, gamma), chained=True)
    while any(left):
        advance(range(chunks))

    def over_aux(value):
        bit = 1
        while bit < parts:
            value = value + lax.ppermute(value, "aux", [(i, i ^ bit) for i in range(parts)])
            bit *= 2
        return value

    early = zero = jnp.zeros((rows, width), F32)
    late = None
    for c in range(chunks):
        g = gamma[c * paux : (c + 1) * paux]
        if isinstance(waiting[c], jax.Array):
            early = sigma_part(g, early, occ[c], waiting[c])
            continue
        shards = waiting[c]
        order = [0]
        for bit in reversed(bits):
            order = order + [d ^ bit for d in order]
        late = zero
        for lo in range(0, fan, fan // ncore):
            some = range(lo, lo + fan // ncore)
            owners = [(z - k) % nz * fan + (index % fan ^ order[d]) for d in some for k in range(nz)]
            some = [v for d in some for v in shards[d]]
            late = sigma_shards(jnp.stack(owners).astype(jnp.int32), g, late, occ[c], some)
    sigma = over_aux(early)
    if late is not None:
        late = late.astype(BF16)
        bit = 1
        while bit < parts:
            got = lax.ppermute(late, "aux", [(i, i ^ bit) for i in range(parts)])
            late = late.astype(F32) + got.astype(F32)
            bit *= 2
            late = late.astype(BF16) if bit < parts else late
        sigma = sigma + late
    return sigma[:, :nint] / math.sqrt(naux * parts * nint)


def solution(mesh):
    in_specs = (P("aux", "ao", None), P("aux", "ao"), P("ao", None), P("ao", None), P())
    out_specs = P("ao", None)
    return jax.shard_map(body, mesh=mesh, in_specs=in_specs, out_specs=out_specs, check_vma=False)
```

```python
import functools
import math

import jax
import jax.numpy as jnp
from jax import lax
from jax.experimental import pallas as pl
from jax.experimental.pallas import tpu as pltpu
from jax.sharding import PartitionSpec as P

BF16, F32 = jnp.bfloat16, jnp.float32
VMEM_BYTES = 50 * 2**20
LANES = 128


def up_to(value, step):
    return -(-value // step) * step


def layout_of(groups):
    core = 2 if groups % 2 == 0 else 1
    chips = groups // core
    x = 1
    while 4 * x * x <= chips and chips % (2 * x) == 0:
        x *= 2
    return chips // x, x, core


def joined(parts_ref, m_ref):
    count, rows, cols = parts_ref.shape
    if cols < m_ref.shape[1]:
        m_ref[:, cols - cols % LANES :] = jnp.zeros((m_ref.shape[0], LANES), BF16)
    for k in range(count):
        m_ref[k * rows : (k + 1) * rows, :cols] = parts_ref[k]


def rows_times(b_ref, m_ref, scale_ref, h_ref):
    mub, paux, naos = b_ref.shape
    step = pl.program_id(0)
    h = jnp.dot(b_ref[...].reshape(mub * paux, naos), m_ref[...], preferred_element_type=F32)
    h = h.reshape(mub, paux, -1) * scale_ref[...]
    h = h.reshape(mub * paux, -1).astype(BF16).astype(F32)
    first = pl.multiple_of(step * (mub * paux), 8)
    for t in range(h_ref.shape[0]):
        h_ref[t, pl.ds(first, mub * paux), :] = h[:, t * LANES : (t + 1) * LANES]


def rows_of(h_ref, p, paux):
    rows = h_ref.shape[1] // paux
    return jnp.concatenate(
        [h_ref[t, pl.ds(p, rows, stride=paux), :] for t in range(h_ref.shape[0])], axis=1
    )


def rot_kernel(paux, fan, nz, cuts, me_ref, b_ref, m_ref, scale_ref, ct_ref, w_ref, tie_ref, *rest):
    outs, gamma_ref, h_ref = rest[:fan], rest[fan], rest[-1]
    if len(m_ref.shape) == 3:
        parts_ref, m_ref = m_ref, rest[fan + 1]
        pl.when(pl.program_id(0) == 0)(lambda: joined(parts_ref, m_ref))
    rows_times(b_ref, m_ref, scale_ref, h_ref)

    @pl.when(pl.program_id(0) == pl.num_programs(0) - 1)
    def _():
        width = ct_ref.shape[0]
        shard = width // cuts
        for d in range(0, fan, cuts):
            wide = []
            for k in range(nz):
                p = (k * fan + jnp.bitwise_xor(me_ref[0], d)) // cuts
                hp = rows_of(h_ref, p, paux)
                gamma_ref[pl.ds(p, 1)] = jnp.sum(hp * w_ref[...], axis=0, keepdims=True)[None]
                wide.append(hp.astype(BF16))
            y = jnp.dot(ct_ref[...], jnp.concatenate(wide, axis=1), preferred_element_type=F32)
            y = y.astype(BF16)
            for k in range(nz):
                for e in range(cuts):
                    outs[d + e][k] = y[e * shard : (e + 1) * shard, k * width : (k + 1) * width]


def occ_kernel(paux, b_ref, m_ref, scale_ref, tie_ref, out_ref, *rest):
    h_ref = rest[-1]
    if len(m_ref.shape) == 3:
        parts_ref, m_ref = m_ref, rest[0]
        pl.when(pl.program_id(0) == 0)(lambda: joined(parts_ref, m_ref))
    rows_times(b_ref, m_ref, scale_ref, h_ref)

    @pl.when(pl.program_id(0) == pl.num_programs(0) - 1)
    def _():
        for p in range(paux):
            out_ref[p] = rows_of(h_ref, p, paux).astype(BF16)


def sigma_kernel(batch, gamma_ref, base_ref, h_ref, y_ref, out_ref):
    step = pl.program_id(0)

    @pl.when(step == 0)
    def _():
        out_ref[...] = base_ref[...]

    h = jnp.concatenate([h_ref[b] for b in range(batch)], axis=1)
    y = y_ref[...].reshape(-1, y_ref.shape[2])
    acc = out_ref[...] - jnp.dot(h, y, preferred_element_type=F32)
    for b in range(batch):
        acc = acc + (2.0 * gamma_ref[step * batch + b]) * h_ref[b].astype(F32)
    out_ref[...] = acc


def shards_kernel(count, owners_ref, gamma_ref, base_ref, h_ref, *rest):
    y_refs, out_ref = rest[:count], rest[count]
    batch = 4 if count % 4 == 0 else 1
    acc = base_ref[...]
    for first in range(0, count, batch):
        some = range(first, first + batch)
        h = [h_ref[owners_ref[i]] for i in some]
        y = jnp.concatenate([y_refs[i][...] for i in some], axis=0)
        acc = acc - jnp.dot(jnp.concatenate(h, axis=1), y, preferred_element_type=F32)
        for i, one in zip(some, h):
            acc = acc + (2.0 * gamma_ref[owners_ref[i]]) * one.astype(F32)
    out_ref[...] = acc


def cost(flops, nbytes):
    return pl.CostEstimate(flops=flops, bytes_accessed=nbytes, transcendentals=0)


def block_specs(rows, nscale, paux, naos, shape, chunk):
    mub = rows // nscale
    return [
        pl.BlockSpec((mub, paux, naos), lambda s, *_: (s, chunk, 0)),
        pl.BlockSpec(shape, lambda s, *_: (0,) * len(shape), pipeline_mode=pl.Buffered(1)),
        pl.BlockSpec((1, paux, 1), lambda s, *_: (s, chunk, 0)),
    ]


def rot_part(me, blocks, matrix, scale, ct, weighted, tie, chunk, paux, fan, nz, cuts):
    rows, _, naos = blocks.shape
    nscale, width = scale.shape[0], up_to(matrix.shape[-1], LANES)
    extra = [(naos, width)] if matrix.ndim == 3 else []
    piece = jax.ShapeDtypeStruct((nz, width // cuts, width), BF16)

    def whole(shape):
        return pl.BlockSpec(shape, lambda s, *_: (0,) * len(shape))

    return pl.pallas_call(
        functools.partial(rot_kernel, paux, fan, nz, cuts),
        grid_spec=pltpu.PrefetchScalarGridSpec(
            num_scalar_prefetch=1,
            grid=(nscale,),
            in_specs=block_specs(rows, nscale, paux, naos, matrix.shape, chunk)
            + [whole(ct.shape), whole(weighted.shape), pl.BlockSpec(memory_space=pl.ANY)],
            out_specs=[whole(piece.shape)] * fan
            + [whole((paux, 1, width))]
            + [pl.BlockSpec(e, lambda s, *_: (0, 0)) for e in extra],
            scratch_shapes=[pltpu.VMEM((width // LANES, rows * paux, LANES), F32)],
        ),
        out_shape=[piece] * fan
        + [jax.ShapeDtypeStruct((paux, 1, width), F32)]
        + [jax.ShapeDtypeStruct(e, BF16) for e in extra],
        compiler_params=pltpu.CompilerParams(vmem_limit_bytes=VMEM_BYTES),
        cost_estimate=cost(2 * rows * paux * naos * width, 2 * rows * paux * naos),
    )(me, blocks, matrix, scale, ct, weighted, tie)


def occ_part(blocks, matrix, scale, tie, chunk, paux):
    rows, _, naos = blocks.shape
    nscale, width = scale.shape[0], up_to(matrix.shape[-1], LANES)
    extra = [(naos, width)] if matrix.ndim == 3 else []
    out = jax.ShapeDtypeStruct((paux, rows, width), BF16)
    return pl.pallas_call(
        functools.partial(occ_kernel, paux),
        grid=(nscale,),
        in_specs=block_specs(rows, nscale, paux, naos, matrix.shape, chunk)
        + [pl.BlockSpec(memory_space=pl.ANY)],
        out_specs=[pl.BlockSpec(out.shape, lambda s: (0, 0, 0))]
        + [pl.BlockSpec(e, lambda s: (0, 0)) for e in extra],
        out_shape=[out] + [jax.ShapeDtypeStruct(e, BF16) for e in extra],
        scratch_shapes=[pltpu.VMEM((width // LANES, rows * paux, LANES), F32)],
        compiler_params=pltpu.CompilerParams(vmem_limit_bytes=VMEM_BYTES),
        cost_estimate=cost(2 * rows * paux * naos * width, 2 * rows * paux * naos),
    )(blocks, matrix, scale, tie)


def sigma_part(gamma, base, h_occ, ymo):
    paux, width, _ = ymo.shape
    rows = h_occ.shape[1]
    batch = 4 if paux % 4 == 0 else 1
    total = pl.BlockSpec((rows, width), lambda s: (0, 0))
    return pl.pallas_call(
        functools.partial(sigma_kernel, batch),
        grid=(paux // batch,),
        in_specs=[
            pl.BlockSpec(memory_space=pltpu.SMEM),
            total,
            pl.BlockSpec((batch, rows, width), lambda s: (s, 0, 0)),
            pl.BlockSpec((batch, width, width), lambda s: (s, 0, 0)),
        ],
        out_specs=total,
        out_shape=jax.ShapeDtypeStruct((rows, width), F32),
        compiler_params=pltpu.CompilerParams(vmem_limit_bytes=VMEM_BYTES),
        cost_estimate=cost(2 * rows * paux * width * width, 2 * paux * width * width),
    )(gamma, base, h_occ, ymo)


def sigma_shards(owners, gamma, base, h_occ, shards):
    paux, rows, width = h_occ.shape
    return pl.pallas_call(
        functools.partial(shards_kernel, len(shards)),
        in_specs=[pl.BlockSpec(memory_space=pltpu.SMEM)] * 2
        + [pl.BlockSpec(memory_space=pltpu.VMEM)] * (2 + len(shards)),
        out_specs=pl.BlockSpec(memory_space=pltpu.VMEM),
        out_shape=jax.ShapeDtypeStruct((rows, width), F32),
        compiler_params=pltpu.CompilerParams(vmem_limit_bytes=VMEM_BYTES),
        cost_estimate=cost(2 * rows * len(shards) * width * width, 2 * len(shards) * width * width),
    )(owners, gamma, base, h_occ, *shards)


def after(value, others):
    return lax.optimization_barrier((value, others))[0]


def body(blocks, block_scale, coeff, rot_coeff, occupation):
    groups, parts = lax.axis_size("ao"), lax.axis_size("aux")
    nz, nx, ncore = layout_of(groups)
    fan = nx * ncore
    naux, rows, naos = blocks.shape
    nint = coeff.shape[1]
    width = up_to(nint, LANES)
    index = lax.axis_index("ao")
    z = index // fan
    me = jnp.reshape(index % fan, (1,)).astype(jnp.int32)

    def swap(value, bit):
        return lax.ppermute(value, "ao", [(i, i ^ bit) for i in range(groups)])

    def turn_z(value, by):
        return lax.ppermute(value, "ao", [(i, (i + by * fan) % groups) for i in range(groups)])

    def along_z(value, pairs):
        return lax.ppermute(
            value, "ao", [(a * fan + i, b * fan + i) for a, b in pairs for i in range(fan)]
        )

    def line_z(mine):
        if nz != 4:
            return [mine] + [turn_z(mine, d) for d in range(1, nz)]
        up = along_z(mine, [(0, 1), (1, 2), (2, 3)])
        down = along_z(mine, [(3, 2), (2, 1), (1, 0)])
        near, up, down = lax.optimization_barrier((jnp.where(z < 2, down, up), up, down))
        up2 = along_z(up, [(1, 2), (2, 3)])
        down2 = along_z(down, [(2, 1), (1, 0)])
        far = jnp.where(z < 2, down2, up2)
        last = along_z(far, [(2, 3), (1, 0)])
        other = jnp.where(z == 1, up, jnp.where(z == 2, down, last))
        return [mine, near, far, other]

    if nz == 4:
        from_z = [z, jnp.where(z < 2, z + 1, z - 1), z ^ 2, jnp.where(z % 2 == 0, 3, 0)]
    else:
        from_z = [(z - d) % nz for d in range(nz)]

    def pick(value, k):
        return lax.dynamic_index_in_dim(value, k % nz, 0, keepdims=False)

    paux = 16 if naux % 16 == 0 else naux
    chunks = naux // paux
    cuts = groups // paux

    by_rows = blocks.transpose(1, 0, 2)
    scale = block_scale.T[:, :, None]
    ct = jnp.pad(coeff.T, ((0, width - nint), (0, 0))).reshape(cuts, width // cuts, rows)
    ct = jnp.concatenate(
        [lax.dynamic_index_in_dim(ct, index % cuts ^ e, 0, keepdims=False) for e in range(cuts)]
    )
    weighted = jnp.pad(coeff.astype(F32) * occupation[None, :], ((0, 0), (0, width - nint)))
    whole_r = lax.all_gather(rot_coeff, "ao", axis=0)
    whole_c = lax.all_gather(coeff, "ao", axis=0)
    bits = [1 << k for k in range(fan.bit_length() - 1)]

    def reduce_steps(first, by_permutes):
        live = dict(enumerate(first))
        for bit in bits:
            sent = {d: swap(v, bit) for d, v in live.items() if d & bit}
            sent = yield sent, list(live.values())
            live = {d: v + sent[d | bit] for d, v in live.items() if not d & bit}
        mine = live[0]
        sent = [pick(mine, z + d) for d in range(1, nz)]
        got = yield [turn_z(v, d + 1) for d, v in enumerate(sent)], sent
        total = pick(mine, z).astype(F32)
        for part in got:
            total = total + part.astype(F32)
        total = total.astype(BF16)
        if not by_permutes:
            whole = lax.all_gather(total, "ao", axis=0, tiled=True)
            yield whole.reshape(paux, width, width), total
            return
        shards = [line_z(total)]
        for bit in reversed(bits):
            shards = shards + [[swap(v, bit) for v in column] for column in shards]
        yield shards, total

    flows, waiting, occ, gammas = [], [], [], []
    start = jnp.zeros((8, LANES), F32)

    left = [len(bits) + 1] * chunks

    def in_transit(c):
        return left[c] > 0

    def advance(which, done=()):
        which = [c for c in which if in_transit(c)]
        arrived = after([waiting[c] for c in which], done)
        for c, got in zip(which, arrived):
            waiting[c], marks[c] = flows[c].send(got)
            left[c] -= 1

    marks = {}
    for c in range(chunks):
        out = rot_part(
            me, by_rows, whole_r, scale, ct, weighted, after(start, marks), c, paux, fan, nz, cuts
        )
        first, g = out[:fan], out[fan]
        if c == 0:
            whole_r = out[fan + 1]
        gammas.append(g)
        flows.append(reduce_steps(first, cuts == 1 and c == chunks - 1 > 0))
        got, marks[c] = next(flows[c])
        waiting.append(got)
        advance(range(c + 1), g)
    gamma = jnp.sum(jnp.concatenate(gammas, axis=0), axis=(1, 2))
    hops = [
        [functools.partial(swap, bit=d) for d in range(1, fan)],
        [functools.partial(turn_z, by=d) for d in range(1, nz)],
    ]
    for c in range(chunks):
        hop = hops.pop(0) if hops else []
        got = [move(gamma) for move in hop]
        out, *extra = occ_part(by_rows, whole_c, scale, after(start, (marks, gamma)), c, paux)
        if extra:
            whole_c = extra[0]
        occ.append(out)
        for part in after(got, out):
            gamma = gamma + part
        if any(left):
            advance(range(chunks), (out, gamma))
    for hop in hops:
        gamma = functools.reduce(jnp.add, [move(gamma) for move in hop], gamma)
    while any(left):
        advance(range(chunks))

    sigma = jnp.zeros((rows, width), F32)
    for c in range(chunks):
        g = gamma[c * paux : (c + 1) * paux]
        if isinstance(waiting[c], jax.Array):
            sigma = sigma_part(g, sigma, occ[c], waiting[c])
            continue
        shards = waiting[c]
        order = [0]
        for bit in reversed(bits):
            order = order + [d ^ bit for d in order]
        for lo in range(0, fan, fan // ncore):
            some = range(lo, lo + fan // ncore)
            owners = [k * fan + (index % fan ^ order[d]) for d in some for k in from_z]
            sigma = sigma_shards(
                jnp.stack(owners).astype(jnp.int32), g, sigma, occ[c], [v for d in some for v in shards[d]]
            )
    bit = 1
    while bit < parts:
        sigma = sigma + lax.ppermute(sigma, "aux", [(i, i ^ bit) for i in range(parts)])
        bit *= 2
    return sigma[:, :nint] / math.sqrt(naux * parts * nint)


def solution(mesh):
    in_specs = (P("aux", "ao", None), P("aux", "ao"), P("ao", None), P("ao", None), P())
    out_specs = P("ao", None)
    return jax.shard_map(body, mesh=mesh, in_specs=in_specs, out_specs=out_specs, check_vma=False)
```

```python
import functools
import math

import jax
import jax.numpy as jnp
from jax import lax
from jax.experimental import pallas as pl
from jax.experimental.pallas import tpu as pltpu
from jax.sharding import PartitionSpec as P

BF16, F32 = jnp.bfloat16, jnp.float32
VMEM_BYTES = 50 * 2**20
LANES = 128


def up_to(value, step):
    return -(-value // step) * step


def layout_of(groups):
    core = 2 if groups % 2 == 0 else 1
    chips = groups // core
    x = 1
    while 4 * x * x <= chips and chips % (2 * x) == 0:
        x *= 2
    return chips // x, x, core


def joined(parts_ref, m_ref):
    count, rows, cols = parts_ref.shape
    if cols < m_ref.shape[1]:
        m_ref[:, cols - cols % LANES :] = jnp.zeros((m_ref.shape[0], LANES), BF16)
    for k in range(count):
        m_ref[k * rows : (k + 1) * rows, :cols] = parts_ref[k]


def rows_times(b_ref, m_ref, scale_ref, h_ref):
    mub, paux, naos = b_ref.shape
    step = pl.program_id(0)
    h = jnp.dot(b_ref[...].reshape(mub * paux, naos), m_ref[...], preferred_element_type=F32)
    h = h.reshape(mub, paux, -1) * scale_ref[...]
    h = h.reshape(mub * paux, -1).astype(BF16).astype(F32)
    first = pl.multiple_of(step * (mub * paux), 8)
    for t in range(h_ref.shape[0]):
        h_ref[t, pl.ds(first, mub * paux), :] = h[:, t * LANES : (t + 1) * LANES]


def rows_of(h_ref, p, paux):
    rows = h_ref.shape[1] // paux
    return jnp.concatenate(
        [h_ref[t, pl.ds(p, rows, stride=paux), :] for t in range(h_ref.shape[0])], axis=1
    )


def rot_kernel(paux, fan, nz, cuts, me_ref, b_ref, m_ref, scale_ref, ct_ref, w_ref, tie_ref, *rest):
    outs, gamma_ref, h_ref = rest[:fan], rest[fan], rest[-1]
    if len(m_ref.shape) == 3:
        parts_ref, m_ref = m_ref, rest[fan + 1]
        pl.when(pl.program_id(0) == 0)(lambda: joined(parts_ref, m_ref))
    rows_times(b_ref, m_ref, scale_ref, h_ref)

    @pl.when(pl.program_id(0) == pl.num_programs(0) - 1)
    def _():
        width = ct_ref.shape[0]
        shard = width // cuts
        for d in range(0, fan, cuts):
            wide = []
            for k in range(nz):
                p = (k * fan + jnp.bitwise_xor(me_ref[0], d)) // cuts
                hp = rows_of(h_ref, p, paux)
                gamma_ref[pl.ds(p, 1)] = jnp.sum(hp * w_ref[...], axis=0, keepdims=True)[None]
                wide.append(hp.astype(BF16))
            y = jnp.dot(ct_ref[...], jnp.concatenate(wide, axis=1), preferred_element_type=F32)
            y = y.astype(BF16)
            for k in range(nz):
                for e in range(cuts):
                    outs[d + e][k] = y[e * shard : (e + 1) * shard, k * width : (k + 1) * width]


def occ_kernel(paux, b_ref, m_ref, scale_ref, tie_ref, out_ref, *rest):
    h_ref = rest[-1]
    if len(m_ref.shape) == 3:
        parts_ref, m_ref = m_ref, rest[0]
        pl.when(pl.program_id(0) == 0)(lambda: joined(parts_ref, m_ref))
    rows_times(b_ref, m_ref, scale_ref, h_ref)

    @pl.when(pl.program_id(0) == pl.num_programs(0) - 1)
    def _():
        for p in range(paux):
            out_ref[p] = rows_of(h_ref, p, paux).astype(BF16)


def sigma_kernel(batch, gamma_ref, base_ref, h_ref, y_ref, out_ref):
    step = pl.program_id(0)

    @pl.when(step == 0)
    def _():
        out_ref[...] = base_ref[...]

    h = jnp.concatenate([h_ref[b] for b in range(batch)], axis=1)
    y = y_ref[...].reshape(-1, y_ref.shape[2])
    acc = out_ref[...] - jnp.dot(h, y, preferred_element_type=F32)
    for b in range(batch):
        acc = acc + (2.0 * gamma_ref[step * batch + b]) * h_ref[b].astype(F32)
    out_ref[...] = acc


def shards_kernel(count, owners_ref, gamma_ref, base_ref, h_ref, *rest):
    y_refs, out_ref = rest[:count], rest[count]
    batch = 4 if count % 4 == 0 else 1
    acc = base_ref[...]
    for first in range(0, count, batch):
        some = range(first, first + batch)
        h = [h_ref[owners_ref[i]] for i in some]
        y = jnp.concatenate([y_refs[i][...] for i in some], axis=0)
        acc = acc - jnp.dot(jnp.concatenate(h, axis=1), y, preferred_element_type=F32)
        for i, one in zip(some, h):
            acc = acc + (2.0 * gamma_ref[owners_ref[i]]) * one.astype(F32)
    out_ref[...] = acc


def cost(flops, nbytes):
    return pl.CostEstimate(flops=flops, bytes_accessed=nbytes, transcendentals=0)


def block_specs(rows, nscale, paux, naos, shape, chunk):
    mub = rows // nscale
    return [
        pl.BlockSpec((mub, paux, naos), lambda s, *_: (s, chunk, 0)),
        pl.BlockSpec(shape, lambda s, *_: (0,) * len(shape), pipeline_mode=pl.Buffered(1)),
        pl.BlockSpec((1, paux, 1), lambda s, *_: (s, chunk, 0)),
    ]


def rot_part(me, blocks, matrix, scale, ct, weighted, tie, chunk, paux, fan, nz, cuts):
    rows, _, naos = blocks.shape
    nscale, width = scale.shape[0], up_to(matrix.shape[-1], LANES)
    extra = [(naos, width)] if matrix.ndim == 3 else []
    piece = jax.ShapeDtypeStruct((nz, width // cuts, width), BF16)

    def whole(shape):
        return pl.BlockSpec(shape, lambda s, *_: (0,) * len(shape))

    return pl.pallas_call(
        functools.partial(rot_kernel, paux, fan, nz, cuts),
        grid_spec=pltpu.PrefetchScalarGridSpec(
            num_scalar_prefetch=1,
            grid=(nscale,),
            in_specs=block_specs(rows, nscale, paux, naos, matrix.shape, chunk)
            + [whole(ct.shape), whole(weighted.shape), pl.BlockSpec(memory_space=pl.ANY)],
            out_specs=[whole(piece.shape)] * fan
            + [whole((paux, 1, width))]
            + [pl.BlockSpec(e, lambda s, *_: (0, 0)) for e in extra],
            scratch_shapes=[pltpu.VMEM((width // LANES, rows * paux, LANES), F32)],
        ),
        out_shape=[piece] * fan
        + [jax.ShapeDtypeStruct((paux, 1, width), F32)]
        + [jax.ShapeDtypeStruct(e, BF16) for e in extra],
        compiler_params=pltpu.CompilerParams(vmem_limit_bytes=VMEM_BYTES),
        cost_estimate=cost(2 * rows * paux * naos * width, 2 * rows * paux * naos),
    )(me, blocks, matrix, scale, ct, weighted, tie)


def occ_part(blocks, matrix, scale, tie, chunk, paux):
    rows, _, naos = blocks.shape
    nscale, width = scale.shape[0], up_to(matrix.shape[-1], LANES)
    extra = [(naos, width)] if matrix.ndim == 3 else []
    out = jax.ShapeDtypeStruct((paux, rows, width), BF16)
    return pl.pallas_call(
        functools.partial(occ_kernel, paux),
        grid=(nscale,),
        in_specs=block_specs(rows, nscale, paux, naos, matrix.shape, chunk)
        + [pl.BlockSpec(memory_space=pl.ANY)],
        out_specs=[pl.BlockSpec(out.shape, lambda s: (0, 0, 0))]
        + [pl.BlockSpec(e, lambda s: (0, 0)) for e in extra],
        out_shape=[out] + [jax.ShapeDtypeStruct(e, BF16) for e in extra],
        scratch_shapes=[pltpu.VMEM((width // LANES, rows * paux, LANES), F32)],
        compiler_params=pltpu.CompilerParams(vmem_limit_bytes=VMEM_BYTES),
        cost_estimate=cost(2 * rows * paux * naos * width, 2 * rows * paux * naos),
    )(blocks, matrix, scale, tie)


def sigma_part(gamma, base, h_occ, ymo):
    paux, width, _ = ymo.shape
    rows = h_occ.shape[1]
    batch = 4 if paux % 4 == 0 else 1
    total = pl.BlockSpec((rows, width), lambda s: (0, 0))
    return pl.pallas_call(
        functools.partial(sigma_kernel, batch),
        grid=(paux // batch,),
        in_specs=[
            pl.BlockSpec(memory_space=pltpu.SMEM),
            total,
            pl.BlockSpec((batch, rows, width), lambda s: (s, 0, 0)),
            pl.BlockSpec((batch, width, width), lambda s: (s, 0, 0)),
        ],
        out_specs=total,
        out_shape=jax.ShapeDtypeStruct((rows, width), F32),
        compiler_params=pltpu.CompilerParams(vmem_limit_bytes=VMEM_BYTES),
        cost_estimate=cost(2 * rows * paux * width * width, 2 * paux * width * width),
    )(gamma, base, h_occ, ymo)


def sigma_shards(owners, gamma, base, h_occ, shards):
    paux, rows, width = h_occ.shape
    return pl.pallas_call(
        functools.partial(shards_kernel, len(shards)),
        in_specs=[pl.BlockSpec(memory_space=pltpu.SMEM)] * 2
        + [pl.BlockSpec(memory_space=pltpu.VMEM)] * (2 + len(shards)),
        out_specs=pl.BlockSpec(memory_space=pltpu.VMEM),
        out_shape=jax.ShapeDtypeStruct((rows, width), F32),
        compiler_params=pltpu.CompilerParams(vmem_limit_bytes=VMEM_BYTES),
        cost_estimate=cost(2 * rows * len(shards) * width * width, 2 * len(shards) * width * width),
    )(owners, gamma, base, h_occ, *shards)


def after(value, others):
    return lax.optimization_barrier((value, others))[0]


def body(blocks, block_scale, coeff, rot_coeff, occupation):
    groups, parts = lax.axis_size("ao"), lax.axis_size("aux")
    nz, nx, ncore = layout_of(groups)
    fan = nx * ncore
    naux, rows, naos = blocks.shape
    nint = coeff.shape[1]
    width = up_to(nint, LANES)
    index = lax.axis_index("ao")
    z = index // fan
    me = jnp.reshape(index % fan, (1,)).astype(jnp.int32)

    def swap(value, bit):
        return lax.ppermute(value, "ao", [(i, i ^ bit) for i in range(groups)])

    def turn_z(value, by):
        return lax.ppermute(value, "ao", [(i, (i + by * fan) % groups) for i in range(groups)])

    def pick(value, k):
        return lax.dynamic_index_in_dim(value, k % nz, 0, keepdims=False)

    paux = 16 if naux % 16 == 0 else naux
    chunks = naux // paux
    cuts = groups // paux

    by_rows = blocks.transpose(1, 0, 2)
    scale = block_scale.T[:, :, None]
    ct = jnp.pad(coeff.T, ((0, width - nint), (0, 0))).reshape(cuts, width // cuts, rows)
    ct = jnp.concatenate(
        [lax.dynamic_index_in_dim(ct, index % cuts ^ e, 0, keepdims=False) for e in range(cuts)]
    )
    weighted = jnp.pad(coeff.astype(F32) * occupation[None, :], ((0, 0), (0, width - nint)))
    whole_r = lax.all_gather(rot_coeff, "ao", axis=0)
    whole_c = lax.all_gather(coeff, "ao", axis=0)
    bits = [1 << k for k in range(fan.bit_length() - 1)]

    def reduce_steps(first, by_permutes):
        live = dict(enumerate(first))
        for bit in bits:
            sent = {d: swap(v, bit) for d, v in live.items() if d & bit}
            sent = yield sent, list(live.values())
            live = {d: v + sent[d | bit] for d, v in live.items() if not d & bit}
        mine = live[0]
        sent = [pick(mine, z + d) for d in range(1, nz)]
        got = yield [turn_z(v, d + 1) for d, v in enumerate(sent)], sent
        total = pick(mine, z).astype(F32)
        for part in got:
            total = total + part.astype(F32)
        total = total.astype(BF16)
        if not by_permutes:
            whole = lax.all_gather(total, "ao", axis=0, tiled=True)
            yield whole.reshape(paux, width, width), total
            return
        shards = [[total] + [turn_z(total, d) for d in range(1, nz)]]
        for bit in reversed(bits):
            shards = shards + [[swap(v, bit) for v in column] for column in shards]
        yield shards, total

    flows, waiting, occ, gammas = [], [], [], []
    start = jnp.zeros((8, LANES), F32)

    left = [len(bits) + 1] * chunks

    def in_transit(c):
        return left[c] > 0

    def advance(which, done=()):
        which = [c for c in which if in_transit(c)]
        arrived = after([waiting[c] for c in which], done)
        for c, got in zip(which, arrived):
            waiting[c], marks[c] = flows[c].send(got)
            left[c] -= 1

    marks = {}
    for c in range(chunks):
        out = rot_part(
            me, by_rows, whole_r, scale, ct, weighted, after(start, marks), c, paux, fan, nz, cuts
        )
        first, g = out[:fan], out[fan]
        if c == 0:
            whole_r = out[fan + 1]
        gammas.append(g)
        flows.append(reduce_steps(first, cuts == 1 and c == chunks - 1 > 0))
        got, marks[c] = next(flows[c])
        waiting.append(got)
        advance(range(c + 1), g)
    gamma = jnp.sum(jnp.concatenate(gammas, axis=0), axis=(1, 2))
    hops = [
        [functools.partial(swap, bit=d) for d in range(1, fan)],
        [functools.partial(turn_z, by=d) for d in range(1, nz)],
    ]
    for c in range(chunks):
        hop = hops.pop(0) if hops else []
        got = [move(gamma) for move in hop]
        out, *extra = occ_part(by_rows, whole_c, scale, after(start, (marks, gamma)), c, paux)
        if extra:
            whole_c = extra[0]
        occ.append(out)
        for part in after(got, out):
            gamma = gamma + part
        if any(left):
            advance(range(chunks), (out, gamma))
    for hop in hops:
        gamma = functools.reduce(jnp.add, [move(gamma) for move in hop], gamma)
    while any(left):
        advance(range(chunks))

    sigma = jnp.zeros((rows, width), F32)
    for c in range(chunks):
        g = gamma[c * paux : (c + 1) * paux]
        if isinstance(waiting[c], jax.Array):
            sigma = sigma_part(g, sigma, occ[c], waiting[c])
            continue
        shards = waiting[c]
        order = [0]
        for bit in reversed(bits):
            order = order + [d ^ bit for d in order]
        for lo in range(0, fan, fan // ncore):
            some = range(lo, lo + fan // ncore)
            owners = [(z - k) % nz * fan + (index % fan ^ order[d]) for d in some for k in range(nz)]
            sigma = sigma_shards(
                jnp.stack(owners).astype(jnp.int32), g, sigma, occ[c], [v for d in some for v in shards[d]]
            )
    bit = 1
    while bit < parts:
        mine = lax.optimization_barrier(sigma.astype(BF16))
        other = lax.ppermute(mine, "aux", [(i, i ^ bit) for i in range(parts)])
        sigma = mine.astype(F32) + other.astype(F32)
        bit *= 2
    return sigma[:, :nint] / math.sqrt(naux * parts * nint)


def solution(mesh):
    in_specs = (P("aux", "ao", None), P("aux", "ao"), P("ao", None), P("ao", None), P())
    out_specs = P("ao", None)
    return jax.shard_map(body, mesh=mesh, in_specs=in_specs, out_specs=out_specs, check_vma=False)
```

```python
import functools
import math

import jax
import jax.numpy as jnp
from jax import lax
from jax.experimental import pallas as pl
from jax.experimental.pallas import tpu as pltpu
from jax.sharding import PartitionSpec as P

BF16, F32 = jnp.bfloat16, jnp.float32
VMEM_BYTES = 50 * 2**20
LANES = 128


def up_to(value, step):
    return -(-value // step) * step


def layout_of(groups):
    core = 2 if groups % 2 == 0 else 1
    chips = groups // core
    x = 1
    while 4 * x * x <= chips and chips % (2 * x) == 0:
        x *= 2
    return chips // x, x, core


def joined(parts_ref, m_ref):
    count, rows, cols = parts_ref.shape
    if cols < m_ref.shape[1]:
        m_ref[:, cols - cols % LANES :] = jnp.zeros((m_ref.shape[0], LANES), BF16)
    for k in range(count):
        m_ref[k * rows : (k + 1) * rows, :cols] = parts_ref[k]


def rows_times(b_ref, m_ref, scale_ref, h_ref):
    mub, paux, naos = b_ref.shape
    step = pl.program_id(0)
    h = jnp.dot(b_ref[...].reshape(mub * paux, naos), m_ref[...], preferred_element_type=F32)
    h = h.reshape(mub, paux, -1) * scale_ref[...]
    h = h.reshape(mub * paux, -1).astype(BF16).astype(F32)
    first = pl.multiple_of(step * (mub * paux), 8)
    for t in range(h_ref.shape[0]):
        h_ref[t, pl.ds(first, mub * paux), :] = h[:, t * LANES : (t + 1) * LANES]


def rows_of(h_ref, p, paux):
    rows = h_ref.shape[1] // paux
    return jnp.concatenate(
        [h_ref[t, pl.ds(p, rows, stride=paux), :] for t in range(h_ref.shape[0])], axis=1
    )


def rot_kernel(paux, fan, nz, cuts, me_ref, b_ref, m_ref, scale_ref, ct_ref, w_ref, tie_ref, *rest):
    outs, gamma_ref, h_ref = rest[:fan], rest[fan], rest[-1]
    if len(m_ref.shape) == 3:
        parts_ref, m_ref = m_ref, rest[fan + 1]
        pl.when(pl.program_id(0) == 0)(lambda: joined(parts_ref, m_ref))
    rows_times(b_ref, m_ref, scale_ref, h_ref)

    @pl.when(pl.program_id(0) == pl.num_programs(0) - 1)
    def _():
        width = ct_ref.shape[0]
        shard = width // cuts
        for d in range(0, fan, cuts):
            wide = []
            for k in range(nz):
                p = (k * fan + jnp.bitwise_xor(me_ref[0], d)) // cuts
                hp = rows_of(h_ref, p, paux)
                gamma_ref[pl.ds(p, 1)] = jnp.sum(hp * w_ref[...], axis=0, keepdims=True)[None]
                wide.append(hp.astype(BF16))
            y = jnp.dot(ct_ref[...], jnp.concatenate(wide, axis=1), preferred_element_type=F32)
            y = y.astype(BF16)
            for k in range(nz):
                for e in range(cuts):
                    outs[d + e][k] = y[e * shard : (e + 1) * shard, k * width : (k + 1) * width]


def occ_kernel(paux, b_ref, m_ref, scale_ref, tie_ref, out_ref, *rest):
    h_ref = rest[-1]
    if len(m_ref.shape) == 3:
        parts_ref, m_ref = m_ref, rest[0]
        pl.when(pl.program_id(0) == 0)(lambda: joined(parts_ref, m_ref))
    rows_times(b_ref, m_ref, scale_ref, h_ref)

    @pl.when(pl.program_id(0) == pl.num_programs(0) - 1)
    def _():
        for p in range(paux):
            out_ref[p] = rows_of(h_ref, p, paux).astype(BF16)


def sigma_kernel(batch, gamma_ref, base_ref, h_ref, y_ref, out_ref):
    step = pl.program_id(0)

    @pl.when(step == 0)
    def _():
        out_ref[...] = base_ref[...]

    h = jnp.concatenate([h_ref[b] for b in range(batch)], axis=1)
    y = y_ref[...].reshape(-1, y_ref.shape[2])
    acc = out_ref[...] - jnp.dot(h, y, preferred_element_type=F32)
    for b in range(batch):
        acc = acc + (2.0 * gamma_ref[step * batch + b]) * h_ref[b].astype(F32)
    out_ref[...] = acc


def shards_kernel(count, owners_ref, gamma_ref, base_ref, h_ref, *rest):
    y_refs, out_ref = rest[:count], rest[count]
    batch = 4 if count % 4 == 0 else 1
    acc = base_ref[...]
    for first in range(0, count, batch):
        some = range(first, first + batch)
        h = [h_ref[owners_ref[i]] for i in some]
        y = jnp.concatenate([y_refs[i][...] for i in some], axis=0)
        acc = acc - jnp.dot(jnp.concatenate(h, axis=1), y, preferred_element_type=F32)
        for i, one in zip(some, h):
            acc = acc + (2.0 * gamma_ref[owners_ref[i]]) * one.astype(F32)
    out_ref[...] = acc


def cost(flops, nbytes):
    return pl.CostEstimate(flops=flops, bytes_accessed=nbytes, transcendentals=0)


def block_specs(rows, nscale, paux, naos, shape, chunk):
    mub = rows // nscale
    return [
        pl.BlockSpec((mub, paux, naos), lambda s, *_: (s, chunk, 0)),
        pl.BlockSpec(shape, lambda s, *_: (0,) * len(shape), pipeline_mode=pl.Buffered(1)),
        pl.BlockSpec((1, paux, 1), lambda s, *_: (s, chunk, 0)),
    ]


def rot_part(me, blocks, matrix, scale, ct, weighted, tie, chunk, paux, fan, nz, cuts):
    rows, _, naos = blocks.shape
    nscale, width = scale.shape[0], up_to(matrix.shape[-1], LANES)
    extra = [(naos, width)] if matrix.ndim == 3 else []
    piece = jax.ShapeDtypeStruct((nz, width // cuts, width), BF16)

    def whole(shape):
        return pl.BlockSpec(shape, lambda s, *_: (0,) * len(shape))

    return pl.pallas_call(
        functools.partial(rot_kernel, paux, fan, nz, cuts),
        grid_spec=pltpu.PrefetchScalarGridSpec(
            num_scalar_prefetch=1,
            grid=(nscale,),
            in_specs=block_specs(rows, nscale, paux, naos, matrix.shape, chunk)
            + [whole(ct.shape), whole(weighted.shape), pl.BlockSpec(memory_space=pl.ANY)],
            out_specs=[whole(piece.shape)] * fan
            + [whole((paux, 1, width))]
            + [pl.BlockSpec(e, lambda s, *_: (0, 0)) for e in extra],
            scratch_shapes=[pltpu.VMEM((width // LANES, rows * paux, LANES), F32)],
        ),
        out_shape=[piece] * fan
        + [jax.ShapeDtypeStruct((paux, 1, width), F32)]
        + [jax.ShapeDtypeStruct(e, BF16) for e in extra],
        compiler_params=pltpu.CompilerParams(vmem_limit_bytes=VMEM_BYTES),
        cost_estimate=cost(2 * rows * paux * naos * width, 2 * rows * paux * naos),
    )(me, blocks, matrix, scale, ct, weighted, tie)


def occ_part(blocks, matrix, scale, tie, chunk, paux):
    rows, _, naos = blocks.shape
    nscale, width = scale.shape[0], up_to(matrix.shape[-1], LANES)
    extra = [(naos, width)] if matrix.ndim == 3 else []
    out = jax.ShapeDtypeStruct((paux, rows, width), BF16)
    return pl.pallas_call(
        functools.partial(occ_kernel, paux),
        grid=(nscale,),
        in_specs=block_specs(rows, nscale, paux, naos, matrix.shape, chunk)
        + [pl.BlockSpec(memory_space=pl.ANY)],
        out_specs=[pl.BlockSpec(out.shape, lambda s: (0, 0, 0))]
        + [pl.BlockSpec(e, lambda s: (0, 0)) for e in extra],
        out_shape=[out] + [jax.ShapeDtypeStruct(e, BF16) for e in extra],
        scratch_shapes=[pltpu.VMEM((width // LANES, rows * paux, LANES), F32)],
        compiler_params=pltpu.CompilerParams(vmem_limit_bytes=VMEM_BYTES),
        cost_estimate=cost(2 * rows * paux * naos * width, 2 * rows * paux * naos),
    )(blocks, matrix, scale, tie)


def sigma_part(gamma, base, h_occ, ymo):
    paux, width, _ = ymo.shape
    rows = h_occ.shape[1]
    batch = 4 if paux % 4 == 0 else 1
    total = pl.BlockSpec((rows, width), lambda s: (0, 0))
    return pl.pallas_call(
        functools.partial(sigma_kernel, batch),
        grid=(paux // batch,),
        in_specs=[
            pl.BlockSpec(memory_space=pltpu.SMEM),
            total,
            pl.BlockSpec((batch, rows, width), lambda s: (s, 0, 0)),
            pl.BlockSpec((batch, width, width), lambda s: (s, 0, 0)),
        ],
        out_specs=total,
        out_shape=jax.ShapeDtypeStruct((rows, width), F32),
        compiler_params=pltpu.CompilerParams(vmem_limit_bytes=VMEM_BYTES),
        cost_estimate=cost(2 * rows * paux * width * width, 2 * paux * width * width),
    )(gamma, base, h_occ, ymo)


def sigma_shards(owners, gamma, base, h_occ, shards):
    paux, rows, width = h_occ.shape
    return pl.pallas_call(
        functools.partial(shards_kernel, len(shards)),
        in_specs=[pl.BlockSpec(memory_space=pltpu.SMEM)] * 2
        + [pl.BlockSpec(memory_space=pltpu.VMEM)] * (2 + len(shards)),
        out_specs=pl.BlockSpec(memory_space=pltpu.VMEM),
        out_shape=jax.ShapeDtypeStruct((rows, width), F32),
        compiler_params=pltpu.CompilerParams(vmem_limit_bytes=VMEM_BYTES),
        cost_estimate=cost(2 * rows * len(shards) * width * width, 2 * len(shards) * width * width),
    )(owners, gamma, base, h_occ, *shards)


def after(value, others):
    return lax.optimization_barrier((value, others))[0]


def body(blocks, block_scale, coeff, rot_coeff, occupation):
    groups, parts = lax.axis_size("ao"), lax.axis_size("aux")
    nz, nx, ncore = layout_of(groups)
    fan = nx * ncore
    naux, rows, naos = blocks.shape
    nint = coeff.shape[1]
    width = up_to(nint, LANES)
    index = lax.axis_index("ao")
    z = index // fan
    me = jnp.reshape(index % fan, (1,)).astype(jnp.int32)

    def swap(value, bit):
        return lax.ppermute(value, "ao", [(i, i ^ bit) for i in range(groups)])

    def turn_z(value, by):
        return lax.ppermute(value, "ao", [(i, (i + by * fan) % groups) for i in range(groups)])

    def pick(value, k):
        return lax.dynamic_index_in_dim(value, k % nz, 0, keepdims=False)

    paux = 16 if naux % 16 == 0 else naux
    chunks = naux // paux
    cuts = groups // paux

    by_rows = blocks.transpose(1, 0, 2)
    scale = block_scale.T[:, :, None]
    ct = jnp.pad(coeff.T, ((0, width - nint), (0, 0))).reshape(cuts, width // cuts, rows)
    ct = jnp.concatenate(
        [lax.dynamic_index_in_dim(ct, index % cuts ^ e, 0, keepdims=False) for e in range(cuts)]
    )
    weighted = jnp.pad(coeff.astype(F32) * occupation[None, :], ((0, 0), (0, width - nint)))
    whole_r = lax.all_gather(rot_coeff, "ao", axis=0)
    whole_c = lax.all_gather(coeff, "ao", axis=0)
    bits = [1 << k for k in range(fan.bit_length() - 1)]

    def reduce_steps(first, by_permutes):
        live = dict(enumerate(first))
        for bit in bits:
            sent = {d: swap(v, bit) for d, v in live.items() if d & bit}
            sent = yield sent, [v for d, v in live.items() if d & bit]
            live = {d: v + sent[d | bit] for d, v in live.items() if not d & bit}
        mine = live[0]
        sent = [pick(mine, z + d) for d in range(1, nz)]
        got = yield [turn_z(v, d + 1) for d, v in enumerate(sent)], sent
        total = pick(mine, z).astype(F32)
        for part in got:
            total = total + part.astype(F32)
        total = total.astype(BF16)
        if not by_permutes:
            whole = lax.all_gather(total, "ao", axis=0, tiled=True)
            yield whole.reshape(paux, width, width), total
            return
        shards = [[total] + [turn_z(total, d) for d in range(1, nz)]]
        for bit in reversed(bits):
            shards = shards + [[swap(v, bit) for v in column] for column in shards]
        yield shards, total

    flows, waiting, occ, gammas = [], [], [], []
    start = jnp.zeros((8, LANES), F32)

    left = [len(bits) + 1] * chunks

    def in_transit(c):
        return left[c] > 0

    def advance(which, done=()):
        which = [c for c in which if in_transit(c)]
        arrived = after([waiting[c] for c in which], done)
        for c, got in zip(which, arrived):
            waiting[c], marks[c] = flows[c].send(got)
            left[c] -= 1

    marks = {}
    for c in range(chunks):
        out = rot_part(
            me, by_rows, whole_r, scale, ct, weighted, after(start, marks), c, paux, fan, nz, cuts
        )
        first, g = after(out[:fan], waiting), out[fan]
        if c == 0:
            whole_r = out[fan + 1]
        gammas.append(g)
        flows.append(reduce_steps(first, cuts == 1 and c == chunks - 1 > 0))
        got, marks[c] = next(flows[c])
        waiting.append(got)
        advance(range(c + 1), g)
    gamma = jnp.sum(jnp.concatenate(gammas, axis=0), axis=(1, 2))
    hops = [
        [functools.partial(swap, bit=d) for d in range(1, fan)],
        [functools.partial(turn_z, by=d) for d in range(1, nz)],
    ]
    for c in range(chunks):
        hop = hops.pop(0) if hops else []
        got = [move(gamma) for move in hop]
        out, *extra = occ_part(by_rows, whole_c, scale, after(start, (marks, gamma)), c, paux)
        if extra:
            whole_c = extra[0]
        occ.append(out)
        for part in after(got, out):
            gamma = gamma + part
        if any(left):
            advance(range(chunks), (out, gamma))
    for hop in hops:
        gamma = functools.reduce(jnp.add, [move(gamma) for move in hop], gamma)
    while any(left):
        advance(range(chunks))

    sigma = jnp.zeros((rows, width), F32)
    for c in range(chunks):
        g = gamma[c * paux : (c + 1) * paux]
        if isinstance(waiting[c], jax.Array):
            sigma = sigma_part(g, sigma, occ[c], waiting[c])
            continue
        shards = waiting[c]
        order = [0]
        for bit in reversed(bits):
            order = order + [d ^ bit for d in order]
        for lo in range(0, fan, fan // ncore):
            some = range(lo, lo + fan // ncore)
            owners = [(z - k) % nz * fan + (index % fan ^ order[d]) for d in some for k in range(nz)]
            sigma = sigma_shards(
                jnp.stack(owners).astype(jnp.int32), g, sigma, occ[c], [v for d in some for v in shards[d]]
            )
    bit = 1
    while bit < parts:
        mine = lax.optimization_barrier(sigma.astype(BF16))
        other = lax.ppermute(mine, "aux", [(i, i ^ bit) for i in range(parts)])
        sigma = mine.astype(F32) + other.astype(F32)
        bit *= 2
    return sigma[:, :nint] / math.sqrt(naux * parts * nint)


def solution(mesh):
    in_specs = (P("aux", "ao", None), P("aux", "ao"), P("ao", None), P("ao", None), P())
    out_specs = P("ao", None)
    return jax.shard_map(body, mesh=mesh, in_specs=in_specs, out_specs=out_specs, check_vma=False)
```
